32 devices in a mesh: groups: 1, dev: 8 (over y, x, core), head: 4 (over z).
Axes of the slice: x: 2, y: 2, z: 4, core: 2. Of those that a mesh axis runs over, the one named last changes fastest.
Arguments:
- queries: bfloat16 [4, 128, 2048], P(None, ('groups', 'dev'), 'head'), may hold values from -6 to 6
- keys_in: bfloat16 [4, 128, 2048], P(None, ('groups', 'dev'), 'head'), may hold values from -6 to 6
- values_in: bfloat16 [4, 128, 4096], P(None, ('groups', 'dev'), 'head'), may hold values from -6 to 6
- out_gate: bfloat16 [4, 128, 4096], P(None, ('groups', 'dev'), 'head'), may hold values from -6 to 6
- beta_logit: float32 [4, 128, 32], P(None, ('groups', 'dev'), 'head'), may hold values from -6 to 6
- decay_rate: float32 [4, 128, 32], P(None, ('groups', 'dev'), 'head'), may hold values from 0.3 to 1
- states: float32 [128, 32, 128, 128], P(('groups', 'dev'), 'head'), may hold values from -3 to 3
- out_weight: bfloat16 [4096, 2048], P('head'), may hold values from -0.09375 to 0.09375
- head_gain: float32 [128], replicated, may hold values from 0.1 to 1.9
- residual: bfloat16 [4, 128, 2048], P(None, ('groups', 'dev', 'head')), may hold values from -3 to 3
- post_gain: float32 [2048], replicated, may hold values from 0.5 to 1.5
- expert_ids: int32 [4, 128, 10], P(None, 'groups'), may hold values from 0 to 31, all different within a row; in each aligned block of 128 rows (0 to 127, 128 to 255, ..., all dimensions but the last counted through in order) at most 48 rows name the same one
- route_weight: float32 [4, 128, 10], P(None, 'groups'), may hold values from 0.05 to 1
- expert_gate: bfloat16 [32, 2048, 512], P(('dev', 'head')), may hold values from -0.25 to 0.25
- expert_up: bfloat16 [32, 2048, 512], P(('dev', 'head')), may hold values from -0.25 to 0.25
- expert_down: bfloat16 [32, 512, 2048], P(('dev', 'head')), may hold values from -0.25 to 0.25
Outputs:
- layer_out: bfloat16 [4, 128, 2048], P(None, ('groups', 'dev', 'head'))
The draws below stay inside these ranges and needn't reach their ends.
Inputs may be any that keep to these rules, and one draw needn't show every extreme that they name: `expert_ids`: the 10 experts of one request and step differ. In each step no expert is named by more than 48 requests of the group, a bound that some block reaches.
All inputs are finite; a program needn't handle non-finite values.
Results may differ from the reference program's by a relative error of at most 0.0075.
Values may be sent and summed in bfloat16 or wider, within the bound.
No kernel may reach another device: no remote copies, remote signals or barrier semaphores. Data moves between devices by JAX's collectives and lax.ppermute only.
A program may use at most 128 MiB of HBM per device.

```python
import math
import jax
import jax.numpy as jnp
import numpy as np
from jax import lax

D = 2048
QK_HEADS = 16
V_HEADS = 32
HK = 128
HV = 128
FFE = 512
TOPK = 10
STEPS = 4
R = 128
EXPERTS = 32
MOST = 48


def steps_of(stream_key, shape, pieces, least, top_value):
    def one(dim, parts):
        draws = jax.random.uniform(jax.random.fold_in(jax.random.fold_in(stream_key, 6), dim), (parts,), jnp.float32, least / len(pieces), top_value / len(pieces))
        return jnp.repeat(jnp.exp(draws), shape[dim] // parts).reshape((-1,) + (1,) * (len(shape) - dim - 1))

    gain = one(*pieces[0])
    for cut in pieces[1:]:
        gain = gain * one(*cut)
    return gain


def deal_out(stream_key, own, number, rows, amount, top, reach, lean):
    ranking = jax.random.permutation(stream_key, amount)
    crowded, common = portions_of(amount, rows * top, reach, lean, True), portions_of(amount, rows * top, reach, lean, False)
    places = jnp.arange(amount)

    def named(lengths, rotation):
        used = int((lengths > 0).sum())
        fixed = max(1, used // 4)
        shifted = fixed + (places - fixed + rotation * (used - fixed)) % max(1, amount - fixed)
        return jnp.zeros((amount,), jnp.int32).at[ranking[jnp.where(places < fixed, places, shifted)]].set(jnp.asarray(lengths, jnp.int32))

    lengths = jnp.where(number % 4 == 0, named(crowded, number // 4), named(common, number - number // 4 - 1))
    mixed = jax.random.permutation(jax.random.fold_in(own, 3), amount)
    donor, taker = mixed[0:amount // 2 * 2:2], mixed[1:amount // 2 * 2:2]
    margin = jnp.minimum(lengths[donor] - 1, reach - lengths[taker]) // 2
    margin = jnp.where((donor == ranking[0]) | (taker == ranking[0]) | (lengths[taker] == 0), 0, jnp.maximum(margin, 0))
    shifted = jax.random.randint(jax.random.fold_in(own, 4), (amount // 2,), 0, 1 << 20) % (margin + 1)
    lengths = lengths.at[donor].add(-shifted).at[taker].add(shifted)
    items = jnp.searchsorted(jnp.cumsum(lengths), jnp.arange(rows * top), side="right").astype(jnp.int32)
    table = items.reshape(top, rows).T
    table = table[jax.random.permutation(jax.random.fold_in(own, 1), rows)]
    rotation = jax.random.randint(jax.random.fold_in(own, 2), (rows, 1), 0, top)
    return jnp.take_along_axis(table, (jnp.arange(top)[None, :] + rotation) % top, axis=1)


def portions_of(amount, total, bound, slope, full):
    loads = [(1 << 20) // math.isqrt(rank ** slope) + 1 for rank in range(1, amount + 1)]
    largest = bound if full else min(bound, max(-(-total // amount), total * loads[0] // sum(loads)))
    least = 1 if total - largest >= amount - 1 else 0
    given, spare = [largest] + [least] * (amount - 1), total - largest - least * (amount - 1)
    while spare > 0:
        candidates = [i for i in range(1, amount) if given[i] < largest] or [i for i in range(1, amount) if given[i] < bound]
        mass, budget = sum([loads[i] for i in candidates]), spare
        for i in candidates:
            more = min(bound - given[i], max(1, budget * loads[i] // mass), spare)
            given[i] = given[i] + more
            spare = spare - more
    return np.array(given)


def gaussian(own_key, extent, deviation, most, split=(), kind=jnp.bfloat16):
    array = deviation * jax.random.normal(own_key, extent, jnp.float32)
    if split:
        array = array * steps_of(own_key, extent, split, -0.22, 0.18)
    return jnp.clip(array, -most, most).astype(kind)


def setup_inputs(seed: int = 0, part: int = 0) -> dict:
    key_list = jax.random.split(jax.random.key(seed), 17)
    part_keys = jax.random.split(jax.random.fold_in(key_list[16], part), 17)
    queries = gaussian(part_keys[0], (STEPS, R, QK_HEADS * HK), 1.0, 6.0, ((1, 8), (2, 4)))
    keys_in = gaussian(part_keys[1], (STEPS, R, QK_HEADS * HK), 1.0, 6.0, ((1, 8), (2, 4)))
    values_in = gaussian(part_keys[2], (STEPS, R, V_HEADS * HV), 1.0, 6.0, ((1, 8), (2, 4)))
    out_gate = gaussian(part_keys[3], (STEPS, R, V_HEADS * HV), 1.0, 6.0, ((1, 8), (2, 4)))
    beta_logit = gaussian(part_keys[4], (STEPS, R, V_HEADS), 1.0, 6.0, ((1, 8), (2, 4)), jnp.float32)
    decay_rate = jnp.clip(0.3 + 0.7 * jax.random.uniform(part_keys[5], (STEPS, R, V_HEADS), jnp.float32) ** steps_of(part_keys[5], (STEPS, R, V_HEADS), ((1, 8), (2, 4)), -0.2, 0.2), 0.3, 1.0)
    states = gaussian(part_keys[6], (R, V_HEADS, HK, HV), 0.5, 3.0, ((0, 8), (1, 4)), jnp.float32)
    out_weight = gaussian(key_list[7], (V_HEADS * HV, D), (V_HEADS * HV) ** -0.5, 0.09375, ((0, 4),))
    head_gain = jnp.clip(1.0 + 0.18 * jax.random.normal(key_list[8], (HV,), jnp.float32), 0.1, 1.9)
    residual = gaussian(part_keys[9], (STEPS, R, D), 0.5, 3.0, ((1, 32),))
    post_gain = jnp.clip(1.0 + 0.1 * jax.random.normal(key_list[10], (D,), jnp.float32), 0.5, 1.5)
    expert_ids_keys = jax.random.split(jax.random.fold_in(part_keys[11], 1), STEPS * R // R)
    expert_ids_turns = jax.random.permutation(jax.random.fold_in(part_keys[11], 3), STEPS * R // R)
    expert_ids = jax.vmap(lambda own, number: deal_out(jax.random.fold_in(part_keys[11], 2), own, number, R, EXPERTS, TOPK, MOST, 2))(expert_ids_keys, expert_ids_turns).reshape((STEPS, R, TOPK))
    route_weight = jnp.clip(jnp.exp(jax.random.uniform(part_keys[12], (STEPS, R, TOPK), jnp.float32, math.log(0.05), math.log(1.0))), 0.05, 1.0)
    expert_gate = gaussian(key_list[13], (EXPERTS, D, FFE), (D // 4) ** -0.5, 0.25, ((0, 32),))
    expert_up = gaussian(key_list[14], (EXPERTS, D, FFE), (D // 4) ** -0.5, 0.25, ((0, 32),))
    expert_down = gaussian(key_list[15], (EXPERTS, FFE, D), FFE ** -0.5, 0.25, ((0, 32),))
    return dict(queries=queries, keys_in=keys_in, values_in=values_in, out_gate=out_gate, beta_logit=beta_logit, decay_rate=decay_rate, states=states, out_weight=out_weight, head_gain=head_gain, residual=residual, post_gain=post_gain, expert_ids=expert_ids, route_weight=route_weight, expert_gate=expert_gate, expert_up=expert_up, expert_down=expert_down)


def unit_rows(values):
    return values * lax.rsqrt(lax.optimization_barrier(jnp.sum(values * values, axis=-1, keepdims=True)) + 1e-06)

def rms_scale(values):
    return values * lax.rsqrt(lax.optimization_barrier(jnp.mean(values * values, axis=-1, keepdims=True)) + 1e-06)

def expert_mlp(rows, gate_mat, up_mat, down_mat):
    gated = jnp.dot(rows, gate_mat, preferred_element_type=jnp.float32)
    lifted = jnp.dot(rows, up_mat, preferred_element_type=jnp.float32)
    hidden = (jax.nn.silu(gated) * lifted).astype(jnp.bfloat16)
    return jnp.dot(hidden, down_mat, preferred_element_type=jnp.float32).astype(jnp.bfloat16)

def mixture(normed, step_ids, step_shares, expert_gate, expert_up, expert_down):

    def visit_expert(totals, packed):
        expert_index, gate_mat, up_mat, down_mat = packed
        matches = step_ids == expert_index
        chosen = jnp.any(matches, axis=-1)
        picked_share = lax.optimization_barrier(jnp.sum(jnp.where(matches, step_shares, 0.0), axis=-1))
        slot_rows = jnp.nonzero(chosen, size=MOST, fill_value=0)[0].astype(jnp.int32)
        filled = jnp.arange(MOST) < jnp.sum(chosen.astype(jnp.int32))
        picked = jnp.take(normed, slot_rows, axis=0)
        served = expert_mlp(picked, gate_mat, up_mat, down_mat).astype(jnp.float32)
        scaled = served * jnp.where(filled, jnp.take(picked_share, slot_rows), 0.0)[:, None]
        return (totals.at[slot_rows].add(scaled), None)
    start_totals = jnp.zeros((normed.shape[0], D), jnp.float32)
    totals, _ = lax.scan(visit_expert, start_totals, (jnp.arange(EXPERTS, dtype=jnp.int32), expert_gate, expert_up, expert_down))
    return totals

def reference(queries, keys_in, values_in, out_gate, beta_logit, decay_rate, states, out_weight, head_gain, residual, post_gain, expert_ids, route_weight, expert_gate, expert_up, expert_down):
    highest = lax.Precision.HIGHEST
    repeat_count = V_HEADS // QK_HEADS
    memory = states
    results = []
    for moment in range(STEPS):
        query_rows = unit_rows(queries[moment].astype(jnp.float32).reshape(R, QK_HEADS, HK)) * HK ** (-0.5)
        query_rows = jnp.repeat(query_rows, repeat_count, axis=1)
        key_rows = jnp.repeat(unit_rows(keys_in[moment].astype(jnp.float32).reshape(R, QK_HEADS, HK)), repeat_count, axis=1)
        value_rows = values_in[moment].astype(jnp.float32).reshape(R, V_HEADS, HV)
        gate_rows = out_gate[moment].astype(jnp.float32).reshape(R, V_HEADS, HV)
        beta_rows = jax.nn.sigmoid(beta_logit[moment])
        memory = memory * decay_rate[moment][:, :, None, None]
        recalled = jnp.einsum('rhk,rhkv->rhv', key_rows, memory, precision=highest)
        delta_rows = (value_rows - recalled) * beta_rows[:, :, None]
        memory = memory + key_rows[:, :, :, None] * delta_rows[:, :, None, :]
        read_out = jnp.einsum('rhk,rhkv->rhv', query_rows, memory, precision=highest)
        gated = rms_scale(read_out) * head_gain * jax.nn.silu(gate_rows)
        flattened = gated.reshape(R, V_HEADS * HV).astype(jnp.bfloat16)
        stream = residual[moment].astype(jnp.float32) + jnp.dot(flattened, out_weight, preferred_element_type=jnp.float32)
        normed = (rms_scale(stream) * post_gain).astype(jnp.bfloat16)
        shares = route_weight[moment] / lax.optimization_barrier(jnp.sum(route_weight[moment], axis=-1, keepdims=True))
        routed = mixture(normed, expert_ids[moment], shares, expert_gate, expert_up, expert_down)
        results.append((stream + routed).astype(jnp.bfloat16))
    return jnp.stack(results)
```

```python
import functools

import jax
import jax.numpy as jnp
from jax import lax
from jax.experimental import pallas as pl
from jax.experimental.pallas import tpu as pltpu
from jax.sharding import PartitionSpec as P

HK = 128
HV = 128
EPS = 1e-06


def attend_kernel(
    place,
    q_ref,
    k_ref,
    v_ref,
    gate_ref,
    beta_ref,
    decay_ref,
    gain_ref,
    states_hbm,
    weight_hbm,
    *rest,
    blocks,
):
    own_ref, send_refs = rest[0], rest[1:blocks]
    state, weight, rows, reads, gated, state_sems, weight_sem = rest[blocks:]
    steps, requests, _ = q_ref.shape
    heads = v_ref.shape[2] // HV
    pairs = q_ref.shape[2] // HK
    repeat = heads // pairs
    each = requests // blocks
    vectors = 2 * steps

    for r in range(requests):
        pltpu.make_async_copy(states_hbm.at[r], state.at[r], state_sems.at[r]).start()
    pltpu.make_async_copy(weight_hbm, weight, weight_sem.at[0]).start()

    unit_q, unit_k = {}, {}
    for g in range(pairs):
        lanes = slice(g * HK, (g + 1) * HK)
        for t in range(steps):
            q = q_ref[t, :, lanes].astype(jnp.float32)
            k = k_ref[t, :, lanes].astype(jnp.float32)
            q = q * lax.rsqrt(jnp.sum(q * q, axis=-1, keepdims=True) + EPS) * HK ** (-0.5)
            k = k * lax.rsqrt(jnp.sum(k * k, axis=-1, keepdims=True) + EPS)
            rows[g, pl.ds(t, requests, stride=vectors), :] = q
            rows[g, pl.ds(steps + t, requests, stride=vectors), :] = k
            unit_q[g, t], unit_k[g, t] = q, k

    def read_states(r, carry):
        pltpu.make_async_copy(states_hbm.at[r], state.at[r], state_sems.at[r]).wait()
        at = pl.ds(pl.multiple_of(r * vectors, vectors), vectors)
        for g in range(pairs):
            left = rows[g, at, :].astype(jnp.bfloat16)
            for h in range(g * repeat, (g + 1) * repeat):
                reads[h, at, :] = jnp.dot(
                    left, state[r, h].astype(jnp.bfloat16), preferred_element_type=jnp.float32
                )
        return carry

    lax.fori_loop(0, requests, read_states, 0)

    for g in range(pairs):
        kk, qk = {}, {}
        for t in range(steps):
            for s in range(t + 1):
                qk[t, s] = jnp.sum(unit_q[g, t] * unit_k[g, s], axis=-1, keepdims=True)
                if s < t:
                    kk[t, s] = jnp.sum(unit_k[g, t] * unit_k[g, s], axis=-1, keepdims=True)
        for h in range(g * repeat, (g + 1) * repeat):
            lanes = slice(h * HV, (h + 1) * HV)
            decay = [decay_ref[t, :, h : h + 1] for t in range(steps)]
            span = {}
            for t in range(steps):
                span[t, t] = None
                for s in range(t - 1, -2, -1):
                    last = span[t, s + 1]
                    span[t, s] = decay[s + 1] if last is None else last * decay[s + 1]
            deltas = []
            for t in range(steps):
                start_q = reads[h, pl.ds(t, requests, stride=vectors), :]
                start_k = reads[h, pl.ds(steps + t, requests, stride=vectors), :]
                recalled = span[t, -1] * start_k
                for s in range(t):
                    recalled = recalled + (span[t, s] * kk[t, s]) * deltas[s]
                beta = jax.nn.sigmoid(beta_ref[t, :, h : h + 1])
                deltas.append((v_ref[t, :, lanes].astype(jnp.float32) - recalled) * beta)
                read = span[t, -1] * start_q
                for s in range(t + 1):
                    factor = qk[t, s] if s == t else span[t, s] * qk[t, s]
                    read = read + factor * deltas[s]
                scale = lax.rsqrt(jnp.mean(read * read, axis=-1, keepdims=True) + EPS)
                gate = gate_ref[t, :, lanes].astype(jnp.float32)
                value = read * scale * gain_ref[...] * jax.nn.silu(gate)
                gated[pl.ds(t * requests, requests), lanes] = value.astype(jnp.bfloat16)

    total = steps * requests
    new = lax.broadcasted_iota(jnp.int32, (total, total), 0)
    old = lax.broadcasted_iota(jnp.int32, (total, total), 1)
    block = new // (steps * each) + place[0]
    block = jnp.where(block >= blocks, block - blocks, block)
    within = new % (steps * each)
    source = (within // each) * requests + block * each + within % each
    chosen = jnp.where(source == old, 1.0, 0.0).astype(jnp.bfloat16)
    ordered = jnp.dot(chosen, gated[...], preferred_element_type=jnp.float32).astype(jnp.bfloat16)

    pltpu.make_async_copy(weight_hbm, weight, weight_sem.at[0]).wait()
    size = steps * each
    columns = weight.shape[1]
    tile = min(512, columns)
    for c in range(0, columns, tile):
        part = jnp.dot(ordered, weight[:, c : c + tile], preferred_element_type=jnp.float32)
        own_ref[:, c : c + tile] = part[:size]
        for k in range(1, blocks):
            send_refs[k - 1][:, c : c + tile] = part[k * size : (k + 1) * size].astype(jnp.bfloat16)


def attend(place, queries, keys_in, values_in, out_gate, beta_logit, decay_rate, gain, states, weight, blocks):
    steps, requests, _ = queries.shape
    heads = values_in.shape[2] // HV
    pairs = queries.shape[2] // HK
    size = steps * requests // blocks
    columns = weight.shape[1]
    whole = pl.BlockSpec(memory_space=pltpu.VMEM)
    away = pl.BlockSpec(memory_space=pl.ANY)
    return pl.pallas_call(
        functools.partial(attend_kernel, blocks=blocks),
        out_shape=[jax.ShapeDtypeStruct((size, columns), jnp.float32)]
        + [jax.ShapeDtypeStruct((size, columns), jnp.bfloat16)] * (blocks - 1),
        in_specs=[pl.BlockSpec(memory_space=pltpu.SMEM)] + [whole] * 7 + [away] * 2,
        out_specs=[whole] * blocks,
        scratch_shapes=[
            pltpu.VMEM(states.shape, jnp.float32),
            pltpu.VMEM(weight.shape, jnp.bfloat16),
            pltpu.VMEM((pairs, requests * 2 * steps, HK), jnp.float32),
            pltpu.VMEM((heads, requests * 2 * steps, HV), jnp.float32),
            pltpu.VMEM((steps * requests, heads * HV), jnp.bfloat16),
            pltpu.SemaphoreType.DMA((requests,)),
            pltpu.SemaphoreType.DMA((1,)),
        ],
        compiler_params=pltpu.CompilerParams(vmem_limit_bytes=32 << 20),
        name="attend",
    )(place, queries, keys_in, values_in, out_gate, beta_logit, decay_rate, gain, states, weight)


def norm_kernel(own_ref, residual_ref, gain_ref, *rest):
    stream_ref, normed_ref = rest[-2:]
    stream = residual_ref[...].astype(jnp.float32) + own_ref[...]
    for ref in rest[:-2]:
        stream = stream + ref[...].astype(jnp.float32)
    stream_ref[...] = stream
    scale = lax.rsqrt(jnp.mean(stream * stream, axis=-1, keepdims=True) + EPS)
    normed_ref[...] = (stream * scale * gain_ref[...]).astype(jnp.bfloat16)


def experts_kernel(x_ref, share_ref, gate_hbm, up_hbm, down_hbm, out_ref, gate, up, down, sems):
    copies = [
        pltpu.make_async_copy(src, dst, sems.at[i])
        for i, (src, dst) in enumerate(((gate_hbm, gate), (up_hbm, up), (down_hbm, down)))
    ]
    for copy in copies:
        copy.start()
    for copy in copies:
        copy.wait()
    count = x_ref.shape[0]
    tile = min(128, count)

    def serve(i, carry):
        at = pl.ds(pl.multiple_of(i * tile, tile), tile)
        x = x_ref[at, :]
        gated = jnp.dot(x, gate[...], preferred_element_type=jnp.float32)
        lifted = jnp.dot(x, up[...], preferred_element_type=jnp.float32)
        hidden = (jax.nn.silu(gated) * lifted).astype(jnp.bfloat16)
        served = jnp.dot(hidden, down[...], preferred_element_type=jnp.float32)
        served = served.astype(jnp.bfloat16).astype(jnp.float32) * share_ref[at, :]
        out_ref[at, :] = served.astype(out_ref.dtype)
        return carry

    lax.fori_loop(0, count // tile, serve, 0)


def experts(x, share, gate, up, down, dtype):
    whole = pl.BlockSpec(memory_space=pltpu.VMEM)
    away = pl.BlockSpec(memory_space=pl.ANY)
    return pl.pallas_call(
        experts_kernel,
        out_shape=jax.ShapeDtypeStruct(x.shape, dtype),
        in_specs=[whole, whole, away, away, away],
        out_specs=whole,
        scratch_shapes=[
            pltpu.VMEM(gate.shape, gate.dtype),
            pltpu.VMEM(up.shape, up.dtype),
            pltpu.VMEM(down.shape, down.dtype),
            pltpu.SemaphoreType.DMA((3,)),
        ],
        compiler_params=pltpu.CompilerParams(vmem_limit_bytes=32 << 20),
        name="experts",
    )(x, share, gate, up, down)


def shards(
    queries,
    keys_in,
    values_in,
    out_gate,
    beta_logit,
    decay_rate,
    states,
    out_weight,
    head_gain,
    residual,
    post_gain,
    expert_ids,
    route_weight,
    expert_gate,
    expert_up,
    expert_down,
):
    ring, width = lax.axis_size("head"), lax.axis_size("dev")
    place, spot = lax.axis_index("head"), lax.axis_index("dev")
    steps, each, columns = residual.shape
    size = steps * each
    bits = (width // 2).bit_length() - 1
    core = spot % 2

    def along(x, k):
        return lax.ppermute(x, "head", [(i, (i + k) % ring) for i in range(ring)])

    def across(x, j):
        return lax.ppermute(
            x, "dev", [(i, i ^ (2 << ((j + i % 2) % bits))) for i in range(width)]
        )

    def other(x):
        return lax.ppermute(x, "dev", [(i, i ^ 1) for i in range(width)])

    def shares_of(spot, core):
        owners = []
        for m in range(1 << bits):
            mask = 0
            for j in range(bits):
                if m >> j & 1:
                    mask = mask + (2 << ((j + core) % bits))
            for k in range(ring):
                owners.append((spot ^ mask) * ring + (place + k) % ring)
        return jnp.stack(owners)

    shares = route_weight / jnp.sum(route_weight, axis=-1, keepdims=True)
    own = spot * ring + place
    picked = jnp.sum(jnp.where(expert_ids == own, shares, 0.0), axis=-1)
    picked = picked.reshape(steps, width * ring, each).transpose(1, 0, 2).reshape(width * ring, size)

    own_shares = jnp.take(picked, shares_of(spot, core), axis=0).reshape(-1, 1)
    peer_shares = jnp.take(picked, shares_of(spot ^ 1, 1 - core), axis=0).reshape(-1, 1)

    parts = attend(
        place.astype(jnp.int32).reshape(1),
        queries,
        keys_in,
        values_in,
        out_gate,
        beta_logit,
        decay_rate,
        head_gain.reshape(1, HV),
        states,
        out_weight,
        ring,
    )
    arrived = [along(parts[k], k) for k in range(1, ring)]
    stream, normed = pl.pallas_call(
        norm_kernel,
        out_shape=[
            jax.ShapeDtypeStruct((size, columns), jnp.float32),
            jax.ShapeDtypeStruct((size, columns), jnp.bfloat16),
        ],
        name="norm",
    )(parts[0], residual.reshape(size, columns), post_gain.reshape(1, columns), *arrived)

    rows = jnp.concatenate([normed] + [along(normed, ring - k) for k in range(1, ring)])
    for j in range(bits):
        rows = jnp.concatenate([rows, across(rows, j)])
    peer_rows = other(rows)
    weights = (expert_gate[0], expert_up[0], expert_down[0])
    peer_served = experts(peer_rows, peer_shares, *weights, jnp.bfloat16)
    served = experts(rows, own_shares, *weights, jnp.float32)
    total = served + other(peer_served).astype(jnp.float32)
    for j in reversed(range(bits)):
        half = total.shape[0] // 2
        total = total[:half] + across(total[half:].astype(jnp.bfloat16), j).astype(jnp.float32)
    routed = stream + total[:size]
    for k in range(1, ring):
        block = total[k * size : (k + 1) * size].astype(jnp.bfloat16)
        routed = routed + along(block, k).astype(jnp.float32)
    return routed.astype(jnp.bfloat16).reshape(steps, each, columns)


def solution(mesh):
    return jax.shard_map(
        shards,
        mesh=mesh,
        in_specs=(
            P(None, ("groups", "dev"), "head"),
            P(None, ("groups", "dev"), "head"),
            P(None, ("groups", "dev"), "head"),
            P(None, ("groups", "dev"), "head"),
            P(None, ("groups", "dev"), "head"),
            P(None, ("groups", "dev"), "head"),
            P(("groups", "dev"), "head", None, None),
            P("head", None),
            P(),
            P(None, ("groups", "dev", "head"), None),
            P(),
            P(None, "groups", None),
            P(None, "groups", None),
            P(("dev", "head"), None, None),
            P(("dev", "head"), None, None),
            P(("dev", "head"), None, None),
        ),
        out_specs=P(None, ("groups", "dev", "head"), None),
        check_vma=False,
    )
```

```python
import functools

import jax
import jax.numpy as jnp
from jax import lax
from jax.experimental import pallas as pl
from jax.experimental.pallas import tpu as pltpu
from jax.sharding import PartitionSpec as P

HK = 128
HV = 128
EPS = 1e-06


def attend_kernel(place, spot, *refs, blocks):
    q_hbm, k_hbm, v_hbm, gate_hbm, beta_hbm, decay_hbm, gain_hbm, states_hbm, weight_hbm = refs[:9]
    expert_hbm, refs = refs[9:12], refs[12:]
    own_ref, send_refs, expert_refs = refs[0], refs[1:blocks], refs[blocks : blocks + 3]
    (q_ref, k_ref, v_ref, gate_ref, beta_ref, decay_ref, gain_ref, state, weight) = refs[
        blocks + 3 : blocks + 12
    ]
    rows, reads, gated, small_sems, state_sems, weight_sems = refs[blocks + 12 :]
    steps, requests, _ = q_ref.shape
    heads = v_ref.shape[2] // HV
    pairs = q_ref.shape[2] // HK
    repeat = heads // pairs
    each = requests // blocks
    vectors = 2 * steps

    small = [
        pltpu.make_async_copy(src, dst, small_sems.at[i])
        for i, (src, dst) in enumerate(
            (
                (q_hbm, q_ref),
                (k_hbm, k_ref),
                (v_hbm, v_ref),
                (gate_hbm, gate_ref),
                (beta_hbm, beta_ref),
                (decay_hbm, decay_ref),
                (gain_hbm, gain_ref),
            )
        )
    ]
    large = [
        pltpu.make_async_copy(src, dst, weight_sems.at[i])
        for i, (src, dst) in enumerate(
            [(weight_hbm, weight)]
            + [(src.at[0], dst) for src, dst in zip(expert_hbm, expert_refs)]
        )
    ]
    for copy in small:
        copy.start()
    for r in range(requests):
        pltpu.make_async_copy(states_hbm.at[r], state.at[r], state_sems.at[r]).start()
    for copy in large:
        copy.start()
    for copy in small:
        copy.wait()

    unit_q, unit_k = {}, {}
    for g in range(pairs):
        lanes = slice(g * HK, (g + 1) * HK)
        for t in range(steps):
            q = q_ref[t, :, lanes].astype(jnp.float32)
            k = k_ref[t, :, lanes].astype(jnp.float32)
            q = q * lax.rsqrt(jnp.sum(q * q, axis=-1, keepdims=True) + EPS) * HK ** (-0.5)
            k = k * lax.rsqrt(jnp.sum(k * k, axis=-1, keepdims=True) + EPS)
            for i, value in ((t, q), (steps + t, k)):
                high = value.astype(jnp.bfloat16).astype(jnp.float32)
                rows[g, pl.ds(i, requests, stride=2 * vectors), :] = high
                rows[g, pl.ds(vectors + i, requests, stride=2 * vectors), :] = value - high
            unit_q[g, t], unit_k[g, t] = q, k

    def read_states(r, carry):
        pltpu.make_async_copy(states_hbm.at[r], state.at[r], state_sems.at[r]).wait()
        both = pl.ds(pl.multiple_of(r * 2 * vectors, 2 * vectors), 2 * vectors)
        at = pl.ds(pl.multiple_of(r * vectors, vectors), vectors)
        for g in range(pairs):
            left = rows[g, both, :].astype(jnp.bfloat16)
            for h in range(g * repeat, (g + 1) * repeat):
                read = jnp.dot(
                    left, state[r, h].astype(jnp.bfloat16), preferred_element_type=jnp.float32
                )
                reads[h, at, :] = read[:vectors] + read[vectors:]
        return carry

    lax.fori_loop(0, requests, read_states, 0)

    betas = jax.nn.sigmoid(beta_ref[...].reshape(steps * heads, requests).T)
    decays = decay_ref[...].reshape(steps * heads, requests).T
    for g in range(pairs):
        kk, qk = {}, {}
        for t in range(steps):
            for s in range(t + 1):
                qk[t, s] = jnp.sum(unit_q[g, t] * unit_k[g, s], axis=-1, keepdims=True)
                if s < t:
                    kk[t, s] = jnp.sum(unit_k[g, t] * unit_k[g, s], axis=-1, keepdims=True)
        for h in range(g * repeat, (g + 1) * repeat):
            lanes = slice(h * HV, (h + 1) * HV)
            decay = [decays[:, t * heads + h : t * heads + h + 1] for t in range(steps)]
            span = {}
            for t in range(steps):
                span[t, t] = None
                for s in range(t - 1, -2, -1):
                    last = span[t, s + 1]
                    span[t, s] = decay[s + 1] if last is None else last * decay[s + 1]
            deltas = []
            for t in range(steps):
                start_q = reads[h, pl.ds(t, requests, stride=vectors), :]
                start_k = reads[h, pl.ds(steps + t, requests, stride=vectors), :]
                recalled = span[t, -1] * start_k
                for s in range(t):
                    recalled = recalled + (span[t, s] * kk[t, s]) * deltas[s]
                beta = betas[:, t * heads + h : t * heads + h + 1]
                deltas.append((v_ref[t, :, lanes].astype(jnp.float32) - recalled) * beta)
                read = span[t, -1] * start_q
                for s in range(t + 1):
                    factor = qk[t, s] if s == t else span[t, s] * qk[t, s]
                    read = read + factor * deltas[s]
                scale = lax.rsqrt(jnp.mean(read * read, axis=-1, keepdims=True) + EPS)
                gate = gate_ref[t, :, lanes].astype(jnp.float32)
                value = read * scale * gain_ref[...] * jax.nn.silu(gate)
                gated[pl.ds(t * requests, requests), lanes] = value.astype(jnp.bfloat16)

    total = steps * requests
    new = lax.broadcasted_iota(jnp.int32, (total, total), 0)
    old = lax.broadcasted_iota(jnp.int32, (total, total), 1)
    block = new // (steps * each) + place[0]
    block = jnp.where(block >= blocks, block - blocks, block)
    within = new % (steps * each)
    source = (within // each) * requests + block * each + within % each
    chosen = jnp.where(source == old, 1.0, 0.0).astype(jnp.bfloat16)
    ordered = jnp.dot(chosen, gated[...], preferred_element_type=jnp.float32).astype(jnp.bfloat16)

    for copy in large:
        copy.wait()
    size = steps * each
    columns = weight.shape[1]
    tile = min(512, columns)
    for c in range(0, columns, tile):
        part = jnp.dot(ordered, weight[:, c : c + tile], preferred_element_type=jnp.float32)
        own_ref[:, c : c + tile] = part[:size]
        for k in range(1, blocks):
            send_refs[k - 1][:, c : c + tile] = part[k * size : (k + 1) * size].astype(jnp.bfloat16)


def attend(place, spot, queries, keys_in, values_in, out_gate, beta, decay, gain, states, weight, mats, blocks):
    steps, requests, _ = queries.shape
    heads = values_in.shape[2] // HV
    pairs = queries.shape[2] // HK
    size = steps * requests // blocks
    columns = weight.shape[1]
    whole = pl.BlockSpec(memory_space=pltpu.VMEM)
    far = pl.BlockSpec(memory_space=pltpu.HBM)
    small = (queries, keys_in, values_in, out_gate, beta, decay, gain)
    return pl.pallas_call(
        functools.partial(attend_kernel, blocks=blocks),
        out_shape=[jax.ShapeDtypeStruct((size, columns), jnp.float32)]
        + [jax.ShapeDtypeStruct((size, columns), jnp.bfloat16)] * (blocks - 1)
        + [pltpu.VMEM(mat.shape[1:], mat.dtype) for mat in mats],
        in_specs=[pl.BlockSpec(memory_space=pltpu.SMEM)] * 2 + [far] * 12,
        out_specs=[whole] * (blocks + 3),
        scratch_shapes=[pltpu.VMEM(x.shape, x.dtype) for x in small]
        + [
            pltpu.VMEM(states.shape, jnp.float32),
            pltpu.VMEM(weight.shape, jnp.bfloat16),
            pltpu.VMEM((pairs, requests * 4 * steps, HK), jnp.float32),
            pltpu.VMEM((heads, requests * 2 * steps, HV), jnp.float32),
            pltpu.VMEM((steps * requests, heads * HV), jnp.bfloat16),
            pltpu.SemaphoreType.DMA((len(small),)),
            pltpu.SemaphoreType.DMA((requests,)),
            pltpu.SemaphoreType.DMA((4,)),
        ],
        compiler_params=pltpu.CompilerParams(vmem_limit_bytes=32 << 20),
        name="attend",
    )(place, spot, *[pltpu.with_memory_space_constraint(x, pltpu.HBM) for x in (*small, states, weight, *mats)])


def local(kernel, out_shape, *operands, name):
    whole = pl.BlockSpec(memory_space=pltpu.VMEM)
    scalars = [x.ndim == 1 for x in operands]
    return pl.pallas_call(
        kernel,
        out_shape=out_shape,
        in_specs=[pl.BlockSpec(memory_space=pltpu.SMEM) if one else whole for one in scalars],
        out_specs=jax.tree.map(lambda _: whole, out_shape),
        compiler_params=pltpu.CompilerParams(vmem_limit_bytes=12 << 20),
        name=name,
    )(*operands)


def norm_kernel(own_ref, residual_ref, gain_ref, *rest):
    arrived, (stream_ref, normed_ref) = rest[:-2], rest[-2:]
    steps, each, _ = residual_ref.shape
    for t in range(steps):
        at = slice(t * each, (t + 1) * each)
        stream_ref[at, :] = residual_ref[t].astype(jnp.float32)
    stream = stream_ref[...] + own_ref[...]
    for ref in arrived:
        stream = stream + ref[...].astype(jnp.float32)
    stream_ref[...] = stream
    scale = lax.rsqrt(jnp.mean(stream * stream, axis=-1, keepdims=True) + EPS)
    normed_ref[...] = (stream * scale * gain_ref[...]).astype(jnp.bfloat16)


def join_kernel(*refs):
    at = 0
    for ref in refs[:-1]:
        refs[-1][pl.ds(at, ref.shape[0]), :] = ref[...]
        at += ref.shape[0]


def join(*parts):
    rows = sum(x.shape[0] for x in parts)
    shape = jax.ShapeDtypeStruct((rows, parts[0].shape[1]), parts[0].dtype)
    return local(join_kernel, shape, *parts, name="join")


def add_kernel(first_ref, second_ref, *outs):
    total = first_ref[...].astype(jnp.float32) + second_ref[...].astype(jnp.float32)
    at = 0
    for out in outs:
        out[...] = total[at : at + out.shape[0]].astype(out.dtype)
        at += out.shape[0]


def add(first, second, *outs):
    shapes = [jax.ShapeDtypeStruct((rows, first.shape[1]), dtype) for rows, dtype in outs]
    return local(add_kernel, shapes, first, second, name="add")


def finish_kernel(stream_ref, own_ref, *rest):
    arrived, out_ref = rest[:-1], rest[-1]
    total = stream_ref[...] + own_ref[...]
    for ref in arrived:
        total = total + ref[...].astype(jnp.float32)
    steps, each, _ = out_ref.shape
    for t in range(steps):
        out_ref[t] = total[t * each : (t + 1) * each].astype(jnp.bfloat16)


def experts_kernel(place, spot, ids_ref, route_ref, gate, up, down, *refs, plan):
    count = len(plan)
    ring, width, bits = plan[0][:3]
    top, steps, requests = ids_ref.shape
    each = requests // (ring * width)
    routes = [route_ref[k] for k in range(top)]
    norm = functools.reduce(jnp.add, routes)
    own = spot[0] * ring + place[0]
    picked = jnp.zeros((steps, requests), jnp.float32)
    for k in range(top):
        picked = picked + jnp.where(ids_ref[k] == own, routes[k] / norm, 0.0)

    for (_, _, _, flip, skip), x_ref, out_ref in zip(plan, refs[:count], refs[count:]):
        rows = x_ref.shape[0]
        row = lax.broadcasted_iota(jnp.int32, (rows, requests), 0) + skip
        column = lax.broadcasted_iota(jnp.int32, (rows, requests), 1)
        size = steps * each
        block = row // size
        k, m = block % ring, block // ring
        device = jnp.bitwise_xor(spot[0], flip)
        core = device % 2
        mask = jnp.zeros_like(row)
        for j in range(bits):
            mask = mask + ((m >> j) & 1) * (jnp.int32(2) << ((j + core) % bits))
        far = place[0] + k
        far = jnp.where(far >= ring, far - ring, far)
        owner = jnp.bitwise_xor(device, mask) * ring + far
        moment = (row % size) // each
        request = owner * each + row % each
        share = jnp.zeros((rows, requests), jnp.float32)
        for t in range(steps):
            share = jnp.where(moment == t, jnp.broadcast_to(picked[t : t + 1], (rows, requests)), share)
        share = jnp.sum(jnp.where(request == column, share, 0.0), axis=-1, keepdims=True)

        x = x_ref[...]
        gated = jnp.dot(x, gate[...], preferred_element_type=jnp.float32)
        lifted = jnp.dot(x, up[...], preferred_element_type=jnp.float32)
        hidden = (jax.nn.silu(gated) * lifted).astype(jnp.bfloat16)
        served = jnp.dot(hidden, down[...], preferred_element_type=jnp.float32)
        served = served.astype(jnp.bfloat16).astype(jnp.float32) * share
        out_ref[...] = served.astype(out_ref.dtype)


def shards(
    queries,
    keys_in,
    values_in,
    out_gate,
    beta_logit,
    decay_rate,
    states,
    out_weight,
    head_gain,
    residual,
    post_gain,
    expert_ids,
    route_weight,
    expert_gate,
    expert_up,
    expert_down,
):
    ring, width = lax.axis_size("head"), lax.axis_size("dev")
    place = lax.axis_index("head").astype(jnp.int32).reshape(1)
    spot = lax.axis_index("dev").astype(jnp.int32).reshape(1)
    steps, each, columns = residual.shape
    size = steps * each
    bits = (width // 2).bit_length() - 1

    def along(x, k):
        return lax.ppermute(x, "head", [(i, (i + k) % ring) for i in range(ring)])

    def across(x, j):
        return lax.ppermute(
            x, "dev", [(i, i ^ (2 << ((j + i % 2) % bits))) for i in range(width)]
        )

    def other(x):
        return lax.ppermute(x, "dev", [(i, i ^ 1) for i in range(width)])

    parts = attend(
        place,
        spot,
        queries,
        keys_in,
        values_in,
        out_gate,
        beta_logit.transpose(0, 2, 1),
        decay_rate.transpose(0, 2, 1),
        head_gain.reshape(1, HV),
        states,
        out_weight,
        (expert_gate, expert_up, expert_down),
        ring,
    )
    arrived = [along(parts[k], k) for k in range(1, ring)]
    stream, normed = local(
        norm_kernel,
        [
            jax.ShapeDtypeStruct((size, columns), jnp.float32),
            jax.ShapeDtypeStruct((size, columns), jnp.bfloat16),
        ],
        parts[0],
        residual,
        post_gain.reshape(1, columns),
        *arrived,
        name="norm",
    )

    ids, route = expert_ids.transpose(2, 0, 1), route_weight.transpose(2, 0, 1)

    def experts(*pieces):
        return local(
            functools.partial(
                experts_kernel,
                plan=tuple((ring, width, bits, flip, skip) for _, _, flip, skip in pieces),
            ),
            [jax.ShapeDtypeStruct(x.shape, dtype) for x, dtype, _, _ in pieces],
            place,
            spot,
            ids,
            route,
            *parts[ring:],
            *[x for x, _, _, _ in pieces],
            name="experts",
        )

    rows = join(normed, *[along(normed, ring - k) for k in range(1, ring)])
    for j in range(bits - 1):
        rows = join(rows, across(rows, j))
    half = rows.shape[0]
    late = across(rows, bits - 1)
    served, peer_served = experts(
        (rows, jnp.float32, 0, 0), (other(rows), jnp.bfloat16, 1, 0)
    )
    peer_served, late = lax.optimization_barrier((peer_served, late))
    total = add(served, other(peer_served), (half, jnp.float32))[0]
    late_served = experts((late, jnp.float32, 0, half))[0]
    peer_late = experts((other(late), jnp.bfloat16, 1, half))[0]
    send = add(late_served, other(peer_late), (half, jnp.bfloat16))[0]
    for j in reversed(range(bits)):
        came = across(send, j)
        if j > 0:
            half //= 2
            total, send = add(total, came, (half, jnp.float32), (half, jnp.bfloat16))
    total, *blocks = add(
        total, came, (size, jnp.float32), *[(size, jnp.bfloat16)] * (ring - 1)
    )
    return local(
        finish_kernel,
        jax.ShapeDtypeStruct((steps, each, columns), jnp.bfloat16),
        stream,
        total,
        *[along(x, k + 1) for k, x in enumerate(blocks)],
        name="finish",
    )


def solution(mesh):
    return jax.shard_map(
        shards,
        mesh=mesh,
        in_specs=(
            P(None, ("groups", "dev"), "head"),
            P(None, ("groups", "dev"), "head"),
            P(None, ("groups", "dev"), "head"),
            P(None, ("groups", "dev"), "head"),
            P(None, ("groups", "dev"), "head"),
            P(None, ("groups", "dev"), "head"),
            P(("groups", "dev"), "head", None, None),
            P("head", None),
            P(),
            P(None, ("groups", "dev", "head"), None),
            P(),
            P(None, "groups", None),
            P(None, "groups", None),
            P(("dev", "head"), None, None),
            P(("dev", "head"), None, None),
            P(("dev", "head"), None, None),
        ),
        out_specs=P(None, ("groups", "dev", "head"), None),
        check_vma=False,
    )
```

```python
import functools

import jax
import jax.numpy as jnp
from jax import lax
from jax.experimental import pallas as pl
from jax.experimental.pallas import tpu as pltpu
from jax.sharding import PartitionSpec as P

HK = 128
HV = 128
EPS = 1e-06


def attend_kernel(place, spot, *refs, blocks):
    q_hbm, k_hbm, v_hbm, gate_hbm, beta_hbm, decay_hbm, gain_hbm, states_hbm, weight_hbm = refs[:9]
    refs = refs[9:]
    own_ref, send_refs = refs[0], refs[1:blocks]
    (q_ref, k_ref, v_ref, gate_ref, beta_ref, decay_ref, gain_ref, state, weight) = refs[
        blocks : blocks + 9
    ]
    rows, reads, gated, small_sems, state_sems, weight_sems = refs[blocks + 9 :]
    steps, requests, _ = q_ref.shape
    heads = v_ref.shape[2] // HV
    pairs = q_ref.shape[2] // HK
    repeat = heads // pairs
    each = requests // blocks
    vectors = 2 * steps

    small = [
        pltpu.make_async_copy(src, dst, small_sems.at[i])
        for i, (src, dst) in enumerate(
            (
                (q_hbm, q_ref),
                (k_hbm, k_ref),
                (v_hbm, v_ref),
                (gate_hbm, gate_ref),
                (beta_hbm, beta_ref),
                (decay_hbm, decay_ref),
                (gain_hbm, gain_ref),
            )
        )
    ]
    large = pltpu.make_async_copy(weight_hbm, weight, weight_sems.at[0])
    for copy in small:
        copy.start()
    for r in range(requests):
        pltpu.make_async_copy(states_hbm.at[r], state.at[r], state_sems.at[r]).start()
    for copy in small:
        copy.wait()

    unit_q, unit_k = {}, {}
    for g in range(pairs):
        lanes = slice(g * HK, (g + 1) * HK)
        for t in range(steps):
            q = q_ref[t, :, lanes].astype(jnp.float32)
            k = k_ref[t, :, lanes].astype(jnp.float32)
            q = q * lax.rsqrt(jnp.sum(q * q, axis=-1, keepdims=True) + EPS) * HK ** (-0.5)
            k = k * lax.rsqrt(jnp.sum(k * k, axis=-1, keepdims=True) + EPS)
            for i, value in ((t, q), (steps + t, k)):
                high = value.astype(jnp.bfloat16).astype(jnp.float32)
                rows[g, pl.ds(i, requests, stride=2 * vectors), :] = high
                rows[g, pl.ds(vectors + i, requests, stride=2 * vectors), :] = value - high
            unit_q[g, t], unit_k[g, t] = q, k

    def read_states(r, carry):
        pltpu.make_async_copy(states_hbm.at[r], state.at[r], state_sems.at[r]).wait()
        both = pl.ds(pl.multiple_of(r * 2 * vectors, 2 * vectors), 2 * vectors)
        at = pl.ds(pl.multiple_of(r * vectors, vectors), vectors)
        for g in range(pairs):
            left = rows[g, both, :].astype(jnp.bfloat16)
            right = [state[r, g * repeat + i].astype(jnp.bfloat16) for i in range(repeat)]
            read = jnp.dot(left, jnp.concatenate(right, axis=1), preferred_element_type=jnp.float32)
            read = read[:vectors] + read[vectors:]
            for i in range(repeat):
                reads[g * repeat + i, at, :] = read[:, i * HV : (i + 1) * HV]
        return carry

    lax.fori_loop(0, requests // 2, read_states, 0)
    large.start()
    lax.fori_loop(requests // 2, requests, read_states, 0)

    betas = jax.nn.sigmoid(beta_ref[...].reshape(steps * heads, requests).T)
    decays = decay_ref[...].reshape(steps * heads, requests).T
    for g in range(pairs):
        kk, qk = {}, {}
        for t in range(steps):
            for s in range(t + 1):
                qk[t, s] = jnp.sum(unit_q[g, t] * unit_k[g, s], axis=-1, keepdims=True)
                if s < t:
                    kk[t, s] = jnp.sum(unit_k[g, t] * unit_k[g, s], axis=-1, keepdims=True)
        for h in range(g * repeat, (g + 1) * repeat):
            lanes = slice(h * HV, (h + 1) * HV)
            decay = [decays[:, t * heads + h : t * heads + h + 1] for t in range(steps)]
            span = {}
            for t in range(steps):
                span[t, t] = None
                for s in range(t - 1, -2, -1):
                    last = span[t, s + 1]
                    span[t, s] = decay[s + 1] if last is None else last * decay[s + 1]
            deltas = []
            for t in range(steps):
                start_q = reads[h, pl.ds(t, requests, stride=vectors), :]
                start_k = reads[h, pl.ds(steps + t, requests, stride=vectors), :]
                recalled = span[t, -1] * start_k
                for s in range(t):
                    recalled = recalled + (span[t, s] * kk[t, s]) * deltas[s]
                beta = betas[:, t * heads + h : t * heads + h + 1]
                deltas.append((v_ref[t, :, lanes].astype(jnp.float32) - recalled) * beta)
                read = span[t, -1] * start_q
                for s in range(t + 1):
                    factor = qk[t, s] if s == t else span[t, s] * qk[t, s]
                    read = read + factor * deltas[s]
                scale = lax.rsqrt(jnp.mean(read * read, axis=-1, keepdims=True) + EPS)
                gate = gate_ref[t, :, lanes].astype(jnp.float32)
                value = read * scale * gain_ref[...] * jax.nn.silu(gate)
                gated[pl.ds(t * requests, requests), lanes] = value.astype(jnp.bfloat16)

    total = steps * requests
    new = lax.broadcasted_iota(jnp.int32, (total, total), 0)
    old = lax.broadcasted_iota(jnp.int32, (total, total), 1)
    block = new // (steps * each) + place[0]
    block = jnp.where(block >= blocks, block - blocks, block)
    within = new % (steps * each)
    source = (within // each) * requests + block * each + within % each
    chosen = jnp.where(source == old, 1.0, 0.0).astype(jnp.bfloat16)
    ordered = jnp.dot(chosen, gated[...], preferred_element_type=jnp.float32).astype(jnp.bfloat16)

    large.wait()
    size = steps * each
    columns = weight.shape[1]
    tile = min(512, columns)
    for c in range(0, columns, tile):
        part = jnp.dot(ordered, weight[:, c : c + tile], preferred_element_type=jnp.float32)
        own_ref[:, c : c + tile] = part[:size]
        for k in range(1, blocks):
            send_refs[k - 1][:, c : c + tile] = part[k * size : (k + 1) * size].astype(jnp.bfloat16)


def attend(place, spot, queries, keys_in, values_in, out_gate, beta, decay, gain, states, weight, blocks):
    steps, requests, _ = queries.shape
    heads = values_in.shape[2] // HV
    pairs = queries.shape[2] // HK
    size = steps * requests // blocks
    columns = weight.shape[1]
    whole = pl.BlockSpec(memory_space=pltpu.VMEM)
    far = pl.BlockSpec(memory_space=pltpu.HBM)
    small = (queries, keys_in, values_in, out_gate, beta, decay, gain)
    return pl.pallas_call(
        functools.partial(attend_kernel, blocks=blocks),
        out_shape=[jax.ShapeDtypeStruct((size, columns), jnp.float32)]
        + [jax.ShapeDtypeStruct((size, columns), jnp.bfloat16)] * (blocks - 1),
        in_specs=[pl.BlockSpec(memory_space=pltpu.SMEM)] * 2 + [far] * 9,
        out_specs=[whole] * blocks,
        scratch_shapes=[pltpu.VMEM(x.shape, x.dtype) for x in small]
        + [
            pltpu.VMEM(states.shape, jnp.float32),
            pltpu.VMEM(weight.shape, jnp.bfloat16),
            pltpu.VMEM((pairs, requests * 4 * steps, HK), jnp.float32),
            pltpu.VMEM((heads, requests * 2 * steps, HV), jnp.float32),
            pltpu.VMEM((steps * requests, heads * HV), jnp.bfloat16),
            pltpu.SemaphoreType.DMA((len(small),)),
            pltpu.SemaphoreType.DMA((requests,)),
            pltpu.SemaphoreType.DMA((1,)),
        ],
        compiler_params=pltpu.CompilerParams(vmem_limit_bytes=32 << 20),
        name="attend",
    )(place, spot, *[pltpu.with_memory_space_constraint(x, pltpu.HBM) for x in (*small, states, weight)])


def local(kernel, out_shape, *operands, name, scratch=()):
    whole = pl.BlockSpec(memory_space=pltpu.VMEM)
    scalars = [x.ndim == 1 for x in operands]
    return pl.pallas_call(
        kernel,
        out_shape=out_shape,
        in_specs=[pl.BlockSpec(memory_space=pltpu.SMEM) if one else whole for one in scalars],
        out_specs=jax.tree.map(lambda _: whole, out_shape),
        compiler_params=pltpu.CompilerParams(vmem_limit_bytes=12 << 20),
        scratch_shapes=scratch,
        name=name,
    )(*operands)


def norm_kernel(own_ref, residual_ref, gain_ref, *rest):
    arrived, (stream_ref, normed_ref) = rest[:-2], rest[-2:]
    steps, each, _ = residual_ref.shape
    for t in range(steps):
        at = slice(t * each, (t + 1) * each)
        stream_ref[at, :] = residual_ref[t].astype(jnp.float32)
    stream = stream_ref[...] + own_ref[...]
    for ref in arrived:
        stream = stream + ref[...].astype(jnp.float32)
    stream_ref[...] = stream
    scale = lax.rsqrt(jnp.mean(stream * stream, axis=-1, keepdims=True) + EPS)
    normed_ref[...] = (stream * scale * gain_ref[...]).astype(jnp.bfloat16)


def load_kernel(*refs):
    count = len(refs) // 2
    copies = [
        pltpu.make_async_copy(src.at[0], dst, refs[-1].at[i])
        for i, (src, dst) in enumerate(zip(refs[:count], refs[count:-1]))
    ]
    for copy in copies:
        copy.start()
    for copy in copies:
        copy.wait()


def load(*mats):
    return pl.pallas_call(
        load_kernel,
        out_shape=[jax.ShapeDtypeStruct(mat.shape[1:], mat.dtype) for mat in mats],
        in_specs=[pl.BlockSpec(memory_space=pltpu.HBM)] * len(mats),
        out_specs=[pl.BlockSpec(memory_space=pltpu.VMEM)] * len(mats),
        scratch_shapes=[pltpu.SemaphoreType.DMA((len(mats),))],
        compiler_params=pltpu.CompilerParams(vmem_limit_bytes=8 << 20),
        name="load",
    )(*[pltpu.with_memory_space_constraint(mat, pltpu.HBM) for mat in mats])


def join_kernel(*refs):
    at = 0
    for ref in refs[:-1]:
        refs[-1][pl.ds(at, ref.shape[0]), :] = ref[...]
        at += ref.shape[0]


def join(*parts):
    rows = sum(x.shape[0] for x in parts)
    shape = jax.ShapeDtypeStruct((rows, parts[0].shape[1]), parts[0].dtype)
    return local(join_kernel, shape, *parts, name="join")


def add_kernel(*refs, count):
    total = refs[0][...].astype(jnp.float32)
    for ref in refs[1:count]:
        total = total + ref[...].astype(jnp.float32)
    at = 0
    for out in refs[count:]:
        out[...] = total[at : at + out.shape[0]].astype(out.dtype)
        at += out.shape[0]


def add(operands, *outs):
    shapes = [jax.ShapeDtypeStruct((rows, operands[0].shape[1]), dtype) for rows, dtype in outs]
    kernel = functools.partial(add_kernel, count=len(operands))
    return local(kernel, shapes, *operands, name="add")


def finish_kernel(stream_ref, own_ref, *rest):
    arrived, out_ref = rest[:-1], rest[-1]
    total = stream_ref[...] + own_ref[...]
    for ref in arrived:
        total = total + ref[...].astype(jnp.float32)
    steps, each, _ = out_ref.shape
    for t in range(steps):
        out_ref[t] = total[t * each : (t + 1) * each].astype(jnp.bfloat16)


def experts_kernel(place, spot, ids_ref, route_ref, gate, up, down, *refs, plan):
    count = len(plan)
    ring, width, bits = plan[0][:3]
    top, steps, requests = ids_ref.shape
    each = requests // (ring * width)
    size = steps * each
    routes = [route_ref[k] for k in range(top)]
    norm = functools.reduce(jnp.add, routes)
    own = spot[0] * ring + place[0]
    picked = jnp.zeros((steps, requests), jnp.float32)
    for k in range(top):
        picked = picked + jnp.where(ids_ref[k] == own, routes[k] / norm, 0.0)

    rows_ref = refs[-1]
    at = 0
    shares = []
    for (_, _, _, flip, skip), x_ref in zip(plan, refs[:count]):
        rows = x_ref.shape[0]
        rows_ref[pl.ds(at, rows), :] = x_ref[...]
        at += rows
        row = lax.broadcasted_iota(jnp.int32, (rows, requests), 0) + skip
        column = lax.broadcasted_iota(jnp.int32, (rows, requests), 1)
        block = row // size
        k, m = block % ring, block // ring
        device = jnp.bitwise_xor(spot[0], flip)
        core = device % 2
        mask = jnp.zeros_like(row)
        for j in range(bits):
            mask = mask + ((m >> j) & 1) * (jnp.int32(2) << ((j + core) % bits))
        far = place[0] + k
        far = jnp.where(far >= ring, far - ring, far)
        owner = jnp.bitwise_xor(device, mask) * ring + far
        moment = (row % size) // each
        request = owner * each + row % each
        share = jnp.zeros((rows, requests), jnp.float32)
        for t in range(steps):
            share = jnp.where(moment == t, jnp.broadcast_to(picked[t : t + 1], (rows, requests)), share)
        shares.append(jnp.sum(jnp.where(request == column, share, 0.0), axis=-1, keepdims=True))

    x = rows_ref[...]
    gated = jnp.dot(x, gate[...], preferred_element_type=jnp.float32)
    lifted = jnp.dot(x, up[...], preferred_element_type=jnp.float32)
    hidden = (jax.nn.silu(gated) * lifted).astype(jnp.bfloat16)
    served = jnp.dot(hidden, down[...], preferred_element_type=jnp.float32)
    served = served.astype(jnp.bfloat16).astype(jnp.float32)
    at = 0
    for share, out_ref in zip(shares, refs[count : 2 * count]):
        rows = out_ref.shape[0]
        out_ref[...] = (served[at : at + rows] * share).astype(out_ref.dtype)
        at += rows


def shards(
    queries,
    keys_in,
    values_in,
    out_gate,
    beta_logit,
    decay_rate,
    states,
    out_weight,
    head_gain,
    residual,
    post_gain,
    expert_ids,
    route_weight,
    expert_gate,
    expert_up,
    expert_down,
):
    ring, width = lax.axis_size("head"), lax.axis_size("dev")
    place = lax.axis_index("head").astype(jnp.int32).reshape(1)
    spot = lax.axis_index("dev").astype(jnp.int32).reshape(1)
    steps, each, columns = residual.shape
    size = steps * each
    bits = (width // 2).bit_length() - 1

    def along(x, k):
        return lax.ppermute(x, "head", [(i, (i + k) % ring) for i in range(ring)])

    def across(x, j):
        return lax.ppermute(
            x, "dev", [(i, i ^ (2 << ((j + i % 2) % bits))) for i in range(width)]
        )

    def other(x):
        return lax.ppermute(x, "dev", [(i, i ^ 1) for i in range(width)])

    parts = attend(
        place,
        spot,
        queries,
        keys_in,
        values_in,
        out_gate,
        beta_logit.transpose(0, 2, 1),
        decay_rate.transpose(0, 2, 1),
        head_gain.reshape(1, HV),
        states,
        out_weight,
        ring,
    )
    arrived = [along(parts[k], k) for k in range(1, ring)]
    arrived, weights = lax.optimization_barrier(
        (arrived, load(expert_gate, expert_up, expert_down))
    )
    stream, normed = local(
        norm_kernel,
        [
            jax.ShapeDtypeStruct((size, columns), jnp.float32),
            jax.ShapeDtypeStruct((size, columns), jnp.bfloat16),
        ],
        parts[0],
        residual,
        post_gain.reshape(1, columns),
        *arrived,
        name="norm",
    )

    ids, route = expert_ids.transpose(2, 0, 1), route_weight.transpose(2, 0, 1)

    def experts(*pieces):
        return local(
            functools.partial(
                experts_kernel,
                plan=tuple((ring, width, bits, flip, skip) for _, _, flip, skip in pieces),
            ),
            [jax.ShapeDtypeStruct(x.shape, dtype) for x, dtype, _, _ in pieces],
            place,
            spot,
            ids,
            route,
            *weights,
            *[x for x, _, _, _ in pieces],
            name="experts",
            scratch=[pltpu.VMEM((sum(x.shape[0] for x, _, _, _ in pieces), columns), jnp.bfloat16)],
        )

    first = join(normed, *[along(normed, ring - k) for k in range(1, ring)])
    held = first.shape[0]
    last = (1 << bits) - 1
    sets, served, totals = {0: first}, {}, {}
    later = first
    for depth in range(bits + 1):
        group = [m for m in range(last + 1) if m.bit_count() == depth]
        for m in group:
            if m:
                j = m.bit_length() - 1
                sets[m] = across(later if m == 1 << j and j else sets[m - (1 << j)], j)
        if depth:
            before = [m for m in served if m.bit_count() == depth - 1]
            done, got = lax.optimization_barrier(
                ([served[m] for m in before], [sets[m] for m in group])
            )
            served.update(zip(before, done))
            sets.update(zip(group, got))
        for m in group:
            served[m] = experts(
                (sets[m], jnp.float32, 0, m * held), (other(sets[m]), jnp.bfloat16, 1, m * held)
            )
        if depth == 0:
            later, served[0] = lax.optimization_barrier((first, served[0]))
    for m in range(last + 1):
        leaves = m >> (bits - 1)
        totals[m] = add(
            (served[m][0], other(served[m][1])), (held, jnp.bfloat16 if leaves else jnp.float32)
        )[0]
    came = {}
    for j in reversed(range(bits)):
        top = 1 << j
        for m in reversed(range(1, top)):
            leaves = m >> (j - 1)
            totals[m] = add(
                (totals[m], across(totals[m + top], j)),
                (held, jnp.bfloat16 if leaves else jnp.float32),
            )[0]
        if top > 1:
            totals[top], totals[0] = lax.optimization_barrier((totals[top], totals[0]))
        came[j] = across(totals[top], j)
    total, *blocks = add(
        (totals[0], *[came[j] for j in reversed(range(bits))]),
        (size, jnp.float32),
        *[(size, jnp.bfloat16)] * (ring - 1),
    )
    return local(
        finish_kernel,
        jax.ShapeDtypeStruct((steps, each, columns), jnp.bfloat16),
        stream,
        total,
        *[along(x, k + 1) for k, x in enumerate(blocks)],
        name="finish",
    )


def solution(mesh):
    return jax.shard_map(
        shards,
        mesh=mesh,
        in_specs=(
            P(None, ("groups", "dev"), "head"),
            P(None, ("groups", "dev"), "head"),
            P(None, ("groups", "dev"), "head"),
            P(None, ("groups", "dev"), "head"),
            P(None, ("groups", "dev"), "head"),
            P(None, ("groups", "dev"), "head"),
            P(("groups", "dev"), "head", None, None),
            P("head", None),
            P(),
            P(None, ("groups", "dev", "head"), None),
            P(),
            P(None, "groups", None),
            P(None, "groups", None),
            P(("dev", "head"), None, None),
            P(("dev", "head"), None, None),
            P(("dev", "head"), None, None),
        ),
        out_specs=P(None, ("groups", "dev", "head"), None),
        check_vma=False,
    )
```

```python
import functools

import jax
import jax.numpy as jnp
from jax import lax
from jax.experimental import pallas as pl
from jax.experimental.pallas import tpu as pltpu
from jax.sharding import PartitionSpec as P

HK = 128
HV = 128
EPS = 1e-06


def attend_kernel(place, spot, *refs, blocks):
    q_hbm, k_hbm, v_hbm, gate_hbm, beta_hbm, decay_hbm, gain_hbm, states_hbm, weight_hbm = refs[:9]
    refs = refs[9:]
    own_ref, send_refs = refs[0], refs[1:blocks]
    (q_ref, k_ref, v_ref, gate_ref, beta_ref, decay_ref, gain_ref, state, weight) = refs[
        blocks : blocks + 9
    ]
    rows, reads, gated, small_sems, state_sems, weight_sems = refs[blocks + 9 :]
    steps, requests, _ = q_ref.shape
    heads = v_ref.shape[2] // HV
    pairs = q_ref.shape[2] // HK
    repeat = heads // pairs
    each = requests // blocks
    vectors = 2 * steps

    small = [
        pltpu.make_async_copy(src, dst, small_sems.at[i])
        for i, (src, dst) in enumerate(
            (
                (q_hbm, q_ref),
                (k_hbm, k_ref),
                (v_hbm, v_ref),
                (gate_hbm, gate_ref),
                (beta_hbm, beta_ref),
                (decay_hbm, decay_ref),
                (gain_hbm, gain_ref),
            )
        )
    ]
    large = pltpu.make_async_copy(weight_hbm, weight, weight_sems.at[0])
    for copy in small[:2]:
        copy.start()
    for r in range(requests // 2):
        pltpu.make_async_copy(states_hbm.at[r], state.at[r], state_sems.at[r]).start()
    for copy in small[2:]:
        copy.start()
    for copy in small[:2]:
        copy.wait()

    unit_q, unit_k = {}, {}
    for g in range(pairs):
        lanes = slice(g * HK, (g + 1) * HK)
        for t in range(steps):
            q = q_ref[t, :, lanes].astype(jnp.float32)
            k = k_ref[t, :, lanes].astype(jnp.float32)
            q = q * lax.rsqrt(jnp.sum(q * q, axis=-1, keepdims=True) + EPS) * HK ** (-0.5)
            k = k * lax.rsqrt(jnp.sum(k * k, axis=-1, keepdims=True) + EPS)
            for i, value in ((t, q), (steps + t, k)):
                high = value.astype(jnp.bfloat16).astype(jnp.float32)
                rows[g, pl.ds(i, requests, stride=2 * vectors), :] = high
                rows[g, pl.ds(vectors + i, requests, stride=2 * vectors), :] = value - high
            unit_q[g, t], unit_k[g, t] = q, k

    def read_states(r, carry):
        pltpu.make_async_copy(states_hbm.at[r], state.at[r], state_sems.at[r]).wait()

        @pl.when(r < requests // 2)
        def _():
            after = r + requests // 2
            pltpu.make_async_copy(
                states_hbm.at[after], state.at[after], state_sems.at[after]
            ).start()

        both = pl.ds(pl.multiple_of(r * 2 * vectors, 2 * vectors), 2 * vectors)
        at = pl.ds(pl.multiple_of(r * vectors, vectors), vectors)
        for g in range(pairs):
            left = rows[g, both, :].astype(jnp.bfloat16)
            right = [state[r, g * repeat + i].astype(jnp.bfloat16) for i in range(repeat)]
            read = jnp.dot(left, jnp.concatenate(right, axis=1), preferred_element_type=jnp.float32)
            read = read[:vectors] + read[vectors:]
            for i in range(repeat):
                reads[g * repeat + i, at, :] = read[:, i * HV : (i + 1) * HV]
        return carry

    early = requests * 3 // 4
    lax.fori_loop(0, early, read_states, 0)
    large.start()
    lax.fori_loop(early, requests, read_states, 0)

    for copy in small[2:]:
        copy.wait()
    betas = jax.nn.sigmoid(beta_ref[...].reshape(steps * heads, requests).T)
    decays = decay_ref[...].reshape(steps * heads, requests).T
    for g in range(pairs):
        kk, qk = {}, {}
        for t in range(steps):
            for s in range(t + 1):
                qk[t, s] = jnp.sum(unit_q[g, t] * unit_k[g, s], axis=-1, keepdims=True)
                if s < t:
                    kk[t, s] = jnp.sum(unit_k[g, t] * unit_k[g, s], axis=-1, keepdims=True)
        for h in range(g * repeat, (g + 1) * repeat):
            lanes = slice(h * HV, (h + 1) * HV)
            decay = [decays[:, t * heads + h : t * heads + h + 1] for t in range(steps)]
            span = {}
            for t in range(steps):
                span[t, t] = None
                for s in range(t - 1, -2, -1):
                    last = span[t, s + 1]
                    span[t, s] = decay[s + 1] if last is None else last * decay[s + 1]
            deltas = []
            for t in range(steps):
                start_q = reads[h, pl.ds(t, requests, stride=vectors), :]
                start_k = reads[h, pl.ds(steps + t, requests, stride=vectors), :]
                recalled = span[t, -1] * start_k
                for s in range(t):
                    recalled = recalled + (span[t, s] * kk[t, s]) * deltas[s]
                beta = betas[:, t * heads + h : t * heads + h + 1]
                deltas.append((v_ref[t, :, lanes].astype(jnp.float32) - recalled) * beta)
                read = span[t, -1] * start_q
                for s in range(t + 1):
                    factor = qk[t, s] if s == t else span[t, s] * qk[t, s]
                    read = read + factor * deltas[s]
                scale = lax.rsqrt(jnp.mean(read * read, axis=-1, keepdims=True) + EPS)
                gate = gate_ref[t, :, lanes].astype(jnp.float32)
                value = read * scale * gain_ref[...] * jax.nn.silu(gate)
                gated[pl.ds(t * requests, requests), lanes] = value.astype(jnp.bfloat16)

    total = steps * requests
    new = lax.broadcasted_iota(jnp.int32, (total, total), 0)
    old = lax.broadcasted_iota(jnp.int32, (total, total), 1)
    block = new // (steps * each) + place[0]
    block = jnp.where(block >= blocks, block - blocks, block)
    within = new % (steps * each)
    source = (within // each) * requests + block * each + within % each
    chosen = jnp.where(source == old, 1.0, 0.0).astype(jnp.bfloat16)
    ordered = jnp.dot(chosen, gated[...], preferred_element_type=jnp.float32).astype(jnp.bfloat16)

    large.wait()
    size = steps * each
    columns = weight.shape[1]
    tile = min(512, columns)
    for c in range(0, columns, tile):
        part = jnp.dot(ordered, weight[:, c : c + tile], preferred_element_type=jnp.float32)
        own_ref[:, c : c + tile] = part[:size]
        for k in range(1, blocks):
            send_refs[k - 1][:, c : c + tile] = part[k * size : (k + 1) * size].astype(jnp.bfloat16)


def attend(place, spot, queries, keys_in, values_in, out_gate, beta, decay, gain, states, weight, blocks):
    steps, requests, _ = queries.shape
    heads = values_in.shape[2] // HV
    pairs = queries.shape[2] // HK
    size = steps * requests // blocks
    columns = weight.shape[1]
    whole = pl.BlockSpec(memory_space=pltpu.VMEM)
    far = pl.BlockSpec(memory_space=pltpu.HBM)
    small = (queries, keys_in, values_in, out_gate, beta, decay, gain)
    return pl.pallas_call(
        functools.partial(attend_kernel, blocks=blocks),
        out_shape=[jax.ShapeDtypeStruct((size, columns), jnp.float32)]
        + [jax.ShapeDtypeStruct((size, columns), jnp.bfloat16)] * (blocks - 1),
        in_specs=[pl.BlockSpec(memory_space=pltpu.SMEM)] * 2 + [far] * 9,
        out_specs=[whole] * blocks,
        scratch_shapes=[pltpu.VMEM(x.shape, x.dtype) for x in small]
        + [
            pltpu.VMEM(states.shape, jnp.float32),
            pltpu.VMEM(weight.shape, jnp.bfloat16),
            pltpu.VMEM((pairs, requests * 4 * steps, HK), jnp.float32),
            pltpu.VMEM((heads, requests * 2 * steps, HV), jnp.float32),
            pltpu.VMEM((steps * requests, heads * HV), jnp.bfloat16),
            pltpu.SemaphoreType.DMA((len(small),)),
            pltpu.SemaphoreType.DMA((requests,)),
            pltpu.SemaphoreType.DMA((1,)),
        ],
        compiler_params=pltpu.CompilerParams(vmem_limit_bytes=32 << 20),
        name="attend",
    )(place, spot, *[pltpu.with_memory_space_constraint(x, pltpu.HBM) for x in (*small, states, weight)])


def local(kernel, out_shape, *operands, name, scratch=()):
    whole = pl.BlockSpec(memory_space=pltpu.VMEM)
    scalars = [x.ndim == 1 for x in operands]
    return pl.pallas_call(
        kernel,
        out_shape=out_shape,
        in_specs=[pl.BlockSpec(memory_space=pltpu.SMEM) if one else whole for one in scalars],
        out_specs=jax.tree.map(lambda _: whole, out_shape),
        compiler_params=pltpu.CompilerParams(vmem_limit_bytes=12 << 20),
        scratch_shapes=scratch,
        name=name,
    )(*operands)


def norm_kernel(own_ref, residual_ref, gain_ref, *rest):
    arrived, (stream_ref, normed_ref) = rest[:-2], rest[-2:]
    steps, each, _ = residual_ref.shape
    for t in range(steps):
        at = slice(t * each, (t + 1) * each)
        stream_ref[at, :] = residual_ref[t].astype(jnp.float32)
    stream = stream_ref[...] + own_ref[...]
    for ref in arrived:
        stream = stream + ref[...].astype(jnp.float32)
    stream_ref[...] = stream
    scale = lax.rsqrt(jnp.mean(stream * stream, axis=-1, keepdims=True) + EPS)
    normed_ref[...] = (stream * scale * gain_ref[...]).astype(jnp.bfloat16)


def load_kernel(*refs):
    count = len(refs) // 2
    copies = [
        pltpu.make_async_copy(src.at[0], dst, refs[-1].at[i])
        for i, (src, dst) in enumerate(zip(refs[:count], refs[count:-1]))
    ]
    for copy in copies:
        copy.start()
    for copy in copies:
        copy.wait()


def load(*mats):
    return pl.pallas_call(
        load_kernel,
        out_shape=[jax.ShapeDtypeStruct(mat.shape[1:], mat.dtype) for mat in mats],
        in_specs=[pl.BlockSpec(memory_space=pltpu.HBM)] * len(mats),
        out_specs=[pl.BlockSpec(memory_space=pltpu.VMEM)] * len(mats),
        scratch_shapes=[pltpu.SemaphoreType.DMA((len(mats),))],
        compiler_params=pltpu.CompilerParams(vmem_limit_bytes=8 << 20),
        name="load",
    )(*[pltpu.with_memory_space_constraint(mat, pltpu.HBM) for mat in mats])


def join_kernel(*refs):
    at = 0
    for ref in refs[:-1]:
        refs[-1][pl.ds(at, ref.shape[0]), :] = ref[...]
        at += ref.shape[0]


def join(*parts):
    rows = sum(x.shape[0] for x in parts)
    shape = jax.ShapeDtypeStruct((rows, parts[0].shape[1]), parts[0].dtype)
    return local(join_kernel, shape, *parts, name="join")


def add_kernel(*refs, count):
    total = refs[0][...].astype(jnp.float32)
    for ref in refs[1:count]:
        total = total + ref[...].astype(jnp.float32)
    at = 0
    for out in refs[count:]:
        out[...] = total[at : at + out.shape[0]].astype(out.dtype)
        at += out.shape[0]


def add(operands, *outs):
    shapes = [jax.ShapeDtypeStruct((rows, operands[0].shape[1]), dtype) for rows, dtype in outs]
    kernel = functools.partial(add_kernel, count=len(operands))
    return local(kernel, shapes, *operands, name="add")


def finish_kernel(stream_ref, own_ref, *rest):
    arrived, out_ref = rest[:-1], rest[-1]
    total = stream_ref[...] + own_ref[...]
    for ref in arrived:
        total = total + ref[...].astype(jnp.float32)
    steps, each, _ = out_ref.shape
    for t in range(steps):
        out_ref[t] = total[t * each : (t + 1) * each].astype(jnp.bfloat16)


def experts_kernel(place, spot, ids_ref, route_ref, gate, up, down, *refs, plan):
    count = len(plan)
    ring, width, bits = plan[0][:3]
    top, steps, requests = ids_ref.shape
    each = requests // (ring * width)
    size = steps * each
    routes = [route_ref[k] for k in range(top)]
    norm = functools.reduce(jnp.add, routes)
    own = spot[0] * ring + place[0]
    picked = jnp.zeros((steps, requests), jnp.float32)
    for k in range(top):
        picked = picked + jnp.where(ids_ref[k] == own, routes[k] / norm, 0.0)

    rows_ref = refs[-1]
    at = 0
    shares = []
    for (_, _, _, flip, skip), x_ref in zip(plan, refs[:count]):
        rows = x_ref.shape[0]
        rows_ref[pl.ds(at, rows), :] = x_ref[...]
        at += rows
        row = lax.broadcasted_iota(jnp.int32, (rows, requests), 0) + skip
        column = lax.broadcasted_iota(jnp.int32, (rows, requests), 1)
        block = row // size
        k, m = block % ring, block // ring
        device = jnp.bitwise_xor(spot[0], flip)
        core = device % 2
        mask = jnp.zeros_like(row)
        for j in range(bits):
            mask = mask + ((m >> j) & 1) * (jnp.int32(2) << ((j + core) % bits))
        far = place[0] + k
        far = jnp.where(far >= ring, far - ring, far)
        owner = jnp.bitwise_xor(device, mask) * ring + far
        moment = (row % size) // each
        request = owner * each + row % each
        share = jnp.zeros((rows, requests), jnp.float32)
        for t in range(steps):
            share = jnp.where(moment == t, jnp.broadcast_to(picked[t : t + 1], (rows, requests)), share)
        shares.append(jnp.sum(jnp.where(request == column, share, 0.0), axis=-1, keepdims=True))

    x = rows_ref[...]
    gated = jnp.dot(x, gate[...], preferred_element_type=jnp.float32)
    lifted = jnp.dot(x, up[...], preferred_element_type=jnp.float32)
    hidden = (jax.nn.silu(gated) * lifted).astype(jnp.bfloat16)
    served = jnp.dot(hidden, down[...], preferred_element_type=jnp.float32)
    served = served.astype(jnp.bfloat16).astype(jnp.float32)
    at = 0
    for share, out_ref in zip(shares, refs[count : 2 * count]):
        rows = out_ref.shape[0]
        out_ref[...] = (served[at : at + rows] * share).astype(out_ref.dtype)
        at += rows


def shards(
    queries,
    keys_in,
    values_in,
    out_gate,
    beta_logit,
    decay_rate,
    states,
    out_weight,
    head_gain,
    residual,
    post_gain,
    expert_ids,
    route_weight,
    expert_gate,
    expert_up,
    expert_down,
):
    ring, width = lax.axis_size("head"), lax.axis_size("dev")
    place = lax.axis_index("head").astype(jnp.int32).reshape(1)
    spot = lax.axis_index("dev").astype(jnp.int32).reshape(1)
    steps, each, columns = residual.shape
    size = steps * each
    bits = (width // 2).bit_length() - 1

    def along(x, k):
        return lax.ppermute(x, "head", [(i, (i + k) % ring) for i in range(ring)])

    def across(x, j):
        return lax.ppermute(
            x, "dev", [(i, i ^ (2 << ((j + i % 2) % bits))) for i in range(width)]
        )

    def other(x):
        return lax.ppermute(x, "dev", [(i, i ^ 1) for i in range(width)])

    parts = attend(
        place,
        spot,
        queries,
        keys_in,
        values_in,
        out_gate,
        beta_logit.transpose(0, 2, 1),
        decay_rate.transpose(0, 2, 1),
        head_gain.reshape(1, HV),
        states,
        out_weight,
        ring,
    )
    arrived = [along(parts[k], k) for k in range(1, ring)]
    arrived, weights = lax.optimization_barrier(
        (arrived, load(expert_gate, expert_up, expert_down))
    )
    stream, normed = local(
        norm_kernel,
        [
            jax.ShapeDtypeStruct((size, columns), jnp.float32),
            jax.ShapeDtypeStruct((size, columns), jnp.bfloat16),
        ],
        parts[0],
        residual,
        post_gain.reshape(1, columns),
        *arrived,
        name="norm",
    )

    ids, route = expert_ids.transpose(2, 0, 1), route_weight.transpose(2, 0, 1)

    def experts(*pieces):
        return local(
            functools.partial(
                experts_kernel,
                plan=tuple((ring, width, bits, flip, skip) for _, _, flip, skip in pieces),
            ),
            [jax.ShapeDtypeStruct(x.shape, dtype) for x, dtype, _, _ in pieces],
            place,
            spot,
            ids,
            route,
            *weights,
            *[x for x, _, _, _ in pieces],
            name="experts",
            scratch=[pltpu.VMEM((sum(x.shape[0] for x, _, _, _ in pieces), columns), jnp.bfloat16)],
        )

    blocks = [normed] + [along(normed, ring - k) for k in range(1, ring)]
    firsts = [join(*blocks[: ring // 2]), join(*blocks[ring // 2 :])]
    first = join(*firsts)
    held = first.shape[0]
    last = (1 << bits) - 1
    sets, parts, served, totals = {0: first}, {0: firsts}, {}, {}

    def serve(m, peers):
        served[m] = experts((sets[m], jnp.float32, 0, m * held), (peers, jnp.bfloat16, 1, m * held))

    later = first
    for j in range(bits):
        top = 1 << j
        if j < bits - 1 or j == 0:
            parts[top] = [across(x, j) for x in parts[0]]
        else:
            sets[top] = across(later, j)
        if j == 0:
            serve(0, other(first))
            later, served[0], parts[1] = lax.optimization_barrier((first, served[0], parts[1]))
            later = first
        for m in range(1, top):
            parts[m + top] = [across(x, j) for x in parts[m]]
            if m not in served:
                serve(m, other(sets[m]))
                parts[m + top], served[m] = lax.optimization_barrier((parts[m + top], served[m]))
        for m in range(1, 2 * top):
            if m not in sets:
                sets[m] = join(*parts[m])
    for m in range(1 << (bits - 1), last + 1):
        peers = other(sets[m])
        if m > 1 and m - 1 in served:
            peers, served[m - 1] = lax.optimization_barrier((peers, served[m - 1]))
        serve(m, peers)
    for m in range(last + 1):
        leaves = m >> (bits - 1)
        totals[m] = add(
            (served[m][0], other(served[m][1])), (held, jnp.bfloat16 if leaves else jnp.float32)
        )[0]
    came = {}
    for j in reversed(range(bits)):
        top = 1 << j
        for m in reversed(range(1, top)):
            leaves = m >> (j - 1)
            totals[m] = add(
                (totals[m], across(totals[m + top], j)),
                (held, jnp.bfloat16 if leaves else jnp.float32),
            )[0]
        if top > 1:
            totals[top], totals[0] = lax.optimization_barrier((totals[top], totals[0]))
        came[j] = across(totals[top], j)
    total, *blocks = add(
        (totals[0], *[came[j] for j in reversed(range(bits))]),
        (size, jnp.float32),
        *[(size, jnp.bfloat16)] * (ring - 1),
    )
    return local(
        finish_kernel,
        jax.ShapeDtypeStruct((steps, each, columns), jnp.bfloat16),
        stream,
        total,
        *[along(x, k + 1) for k, x in enumerate(blocks)],
        name="finish",
    )


def solution(mesh):
    return jax.shard_map(
        shards,
        mesh=mesh,
        in_specs=(
            P(None, ("groups", "dev"), "head"),
            P(None, ("groups", "dev"), "head"),
            P(None, ("groups", "dev"), "head"),
            P(None, ("groups", "dev"), "head"),
            P(None, ("groups", "dev"), "head"),
            P(None, ("groups", "dev"), "head"),
            P(("groups", "dev"), "head", None, None),
            P("head", None),
            P(),
            P(None, ("groups", "dev", "head"), None),
            P(),
            P(None, "groups", None),
            P(None, "groups", None),
            P(("dev", "head"), None, None),
            P(("dev", "head"), None, None),
            P(("dev", "head"), None, None),
        ),
        out_specs=P(None, ("groups", "dev", "head"), None),
        check_vma=False,
    )
```

```python
import functools

import jax
import jax.numpy as jnp
from jax import lax
from jax.experimental import pallas as pl
from jax.experimental.pallas import tpu as pltpu
from jax.sharding import PartitionSpec as P

HK = 128
HV = 128
EPS = 1e-06
AHEAD = 3


def attend_kernel(place, spot, *refs, blocks):
    q_hbm, k_hbm, v_hbm, gate_hbm, beta_hbm, decay_hbm, gain_hbm, states_hbm, weight_hbm = refs[:9]
    refs = refs[9:]
    own_ref, send_refs = refs[0], refs[1:blocks]
    (q_ref, k_ref, v_ref, gate_ref, beta_ref, decay_ref, gain_ref, state, weight) = refs[
        blocks : blocks + 9
    ]
    rows, reads, gated, small_sems, state_sems, weight_sems = refs[blocks + 9 :]
    steps, requests, _ = q_ref.shape
    heads = v_ref.shape[2] // HV
    pairs = q_ref.shape[2] // HK
    repeat = heads // pairs
    each = requests // blocks
    vectors = 2 * steps

    small = [
        pltpu.make_async_copy(src, dst, small_sems.at[i])
        for i, (src, dst) in enumerate(
            (
                (q_hbm, q_ref),
                (k_hbm, k_ref),
                (v_hbm, v_ref),
                (gate_hbm, gate_ref),
                (beta_hbm, beta_ref),
                (decay_hbm, decay_ref),
                (gain_hbm, gain_ref),
            )
        )
    ]
    large = pltpu.make_async_copy(weight_hbm, weight, weight_sems.at[0])
    for copy in small[:2]:
        copy.start()
    parts = [
        pltpu.make_async_copy(
            states_hbm.at[:, pl.ds(g * repeat, repeat)],
            state.at[:, pl.ds(g * repeat, repeat)],
            state_sems.at[g],
        )
        for g in range(pairs)
    ]
    parts[0].start()
    for copy in small[2:]:
        copy.start()
    for copy in parts[1:AHEAD]:
        copy.start()
    for copy in small[:2]:
        copy.wait()

    unit_q, unit_k = {}, {}
    for g in range(pairs):
        lanes = slice(g * HK, (g + 1) * HK)
        for t in range(steps):
            q = q_ref[t, :, lanes].astype(jnp.float32)
            k = k_ref[t, :, lanes].astype(jnp.float32)
            q = q * lax.rsqrt(jnp.sum(q * q, axis=-1, keepdims=True) + EPS) * HK ** (-0.5)
            k = k * lax.rsqrt(jnp.sum(k * k, axis=-1, keepdims=True) + EPS)
            for i, value in ((t, q), (steps + t, k)):
                high = value.astype(jnp.bfloat16).astype(jnp.float32)
                rows[g, pl.ds(i, requests, stride=2 * vectors), :] = high
                rows[g, pl.ds(vectors + i, requests, stride=2 * vectors), :] = value - high
            unit_q[g, t], unit_k[g, t] = q, k

    def read_states(g, r, carry):
        both = pl.ds(pl.multiple_of(r * 2 * vectors, 2 * vectors), 2 * vectors)
        at = pl.ds(pl.multiple_of(r * vectors, vectors), vectors)
        left = rows[g, both, :].astype(jnp.bfloat16)
        right = [state[r, g * repeat + i].astype(jnp.bfloat16) for i in range(repeat)]
        read = jnp.dot(left, jnp.concatenate(right, axis=1), preferred_element_type=jnp.float32)
        read = read[:vectors] + read[vectors:]
        for i in range(repeat):
            reads[g * repeat + i, at, :] = read[:, i * HV : (i + 1) * HV]
        return carry

    for copy in small[2:]:
        copy.wait()
    betas = jax.nn.sigmoid(beta_ref[...].reshape(steps * heads, requests).T)
    decays = decay_ref[...].reshape(steps * heads, requests).T
    for g in range(pairs):
        parts[g].wait()
        if g + AHEAD < pairs:
            parts[g + AHEAD].start()
        if g == max(pairs - AHEAD, 0):
            large.start()
        lax.fori_loop(0, requests, functools.partial(read_states, g), 0, unroll=True)
        kk, qk = {}, {}
        for t in range(steps):
            for s in range(t + 1):
                qk[t, s] = jnp.sum(unit_q[g, t] * unit_k[g, s], axis=-1, keepdims=True)
                if s < t:
                    kk[t, s] = jnp.sum(unit_k[g, t] * unit_k[g, s], axis=-1, keepdims=True)
        for h in range(g * repeat, (g + 1) * repeat):
            lanes = slice(h * HV, (h + 1) * HV)
            decay = [decays[:, t * heads + h : t * heads + h + 1] for t in range(steps)]
            span = {}
            for t in range(steps):
                span[t, t] = None
                for s in range(t - 1, -2, -1):
                    last = span[t, s + 1]
                    span[t, s] = decay[s + 1] if last is None else last * decay[s + 1]
            deltas = []
            for t in range(steps):
                start_q = reads[h, pl.ds(t, requests, stride=vectors), :]
                start_k = reads[h, pl.ds(steps + t, requests, stride=vectors), :]
                recalled = span[t, -1] * start_k
                for s in range(t):
                    recalled = recalled + (span[t, s] * kk[t, s]) * deltas[s]
                beta = betas[:, t * heads + h : t * heads + h + 1]
                deltas.append((v_ref[t, :, lanes].astype(jnp.float32) - recalled) * beta)
                read = span[t, -1] * start_q
                for s in range(t + 1):
                    factor = qk[t, s] if s == t else span[t, s] * qk[t, s]
                    read = read + factor * deltas[s]
                scale = lax.rsqrt(jnp.mean(read * read, axis=-1, keepdims=True) + EPS)
                gate = gate_ref[t, :, lanes].astype(jnp.float32)
                value = read * scale * gain_ref[...] * jax.nn.silu(gate)
                gated[pl.ds(t * requests, requests), lanes] = value.astype(jnp.bfloat16)

    total = steps * requests
    new = lax.broadcasted_iota(jnp.int32, (total, total), 0)
    old = lax.broadcasted_iota(jnp.int32, (total, total), 1)
    block = new // (steps * each) + place[0]
    block = jnp.where(block >= blocks, block - blocks, block)
    within = new % (steps * each)
    source = (within // each) * requests + block * each + within % each
    chosen = jnp.where(source == old, 1.0, 0.0).astype(jnp.bfloat16)
    ordered = jnp.dot(chosen, gated[...], preferred_element_type=jnp.float32).astype(jnp.bfloat16)

    large.wait()
    size = steps * each
    columns = weight.shape[1]
    tile = min(512, columns)
    for c in range(0, columns, tile):
        part = jnp.dot(ordered, weight[:, c : c + tile], preferred_element_type=jnp.float32)
        own_ref[:, c : c + tile] = part[:size]
        for k in range(1, blocks):
            send_refs[k - 1][:, c : c + tile] = part[k * size : (k + 1) * size].astype(jnp.bfloat16)


def attend(place, spot, queries, keys_in, values_in, out_gate, beta, decay, gain, states, weight, blocks):
    steps, requests, _ = queries.shape
    heads = values_in.shape[2] // HV
    pairs = queries.shape[2] // HK
    size = steps * requests // blocks
    columns = weight.shape[1]
    whole = pl.BlockSpec(memory_space=pltpu.VMEM)
    far = pl.BlockSpec(memory_space=pltpu.HBM)
    small = (queries, keys_in, values_in, out_gate, beta, decay, gain)
    return pl.pallas_call(
        functools.partial(attend_kernel, blocks=blocks),
        out_shape=[jax.ShapeDtypeStruct((size, columns), jnp.float32)]
        + [jax.ShapeDtypeStruct((size, columns), jnp.bfloat16)] * (blocks - 1),
        in_specs=[pl.BlockSpec(memory_space=pltpu.SMEM)] * 2 + [far] * 9,
        out_specs=[whole] * blocks,
        scratch_shapes=[pltpu.VMEM(x.shape, x.dtype) for x in small]
        + [
            pltpu.VMEM(states.shape, jnp.float32),
            pltpu.VMEM(weight.shape, jnp.bfloat16),
            pltpu.VMEM((pairs, requests * 4 * steps, HK), jnp.float32),
            pltpu.VMEM((heads, requests * 2 * steps, HV), jnp.float32),
            pltpu.VMEM((steps * requests, heads * HV), jnp.bfloat16),
            pltpu.SemaphoreType.DMA((len(small),)),
            pltpu.SemaphoreType.DMA((pairs,)),
            pltpu.SemaphoreType.DMA((1,)),
        ],
        compiler_params=pltpu.CompilerParams(vmem_limit_bytes=32 << 20),
        name="attend",
    )(place, spot, *[pltpu.with_memory_space_constraint(x, pltpu.HBM) for x in (*small, states, weight)])


def local(kernel, out_shape, *operands, name, scratch=()):
    whole = pl.BlockSpec(memory_space=pltpu.VMEM)
    scalars = [x.ndim == 1 for x in operands]
    return pl.pallas_call(
        kernel,
        out_shape=out_shape,
        in_specs=[pl.BlockSpec(memory_space=pltpu.SMEM) if one else whole for one in scalars],
        out_specs=jax.tree.map(lambda _: whole, out_shape),
        compiler_params=pltpu.CompilerParams(vmem_limit_bytes=12 << 20),
        scratch_shapes=scratch,
        name=name,
    )(*operands)


def norm_kernel(own_ref, residual_ref, gain_ref, *rest):
    arrived, (stream_ref, normed_ref) = rest[:-2], rest[-2:]
    steps, each, _ = residual_ref.shape
    for t in range(steps):
        at = slice(t * each, (t + 1) * each)
        stream_ref[at, :] = residual_ref[t].astype(jnp.float32)
    stream = stream_ref[...] + own_ref[...]
    for ref in arrived:
        stream = stream + ref[...].astype(jnp.float32)
    stream_ref[...] = stream
    scale = lax.rsqrt(jnp.mean(stream * stream, axis=-1, keepdims=True) + EPS)
    normed_ref[...] = (stream * scale * gain_ref[...]).astype(jnp.bfloat16)


def load_kernel(*refs):
    count = len(refs) // 2
    copies = [
        pltpu.make_async_copy(src.at[0], dst, refs[-1].at[i])
        for i, (src, dst) in enumerate(zip(refs[:count], refs[count:-1]))
    ]
    for copy in copies:
        copy.start()
    for copy in copies:
        copy.wait()


def load(*mats):
    return pl.pallas_call(
        load_kernel,
        out_shape=[jax.ShapeDtypeStruct(mat.shape[1:], mat.dtype) for mat in mats],
        in_specs=[pl.BlockSpec(memory_space=pltpu.HBM)] * len(mats),
        out_specs=[pl.BlockSpec(memory_space=pltpu.VMEM)] * len(mats),
        scratch_shapes=[pltpu.SemaphoreType.DMA((len(mats),))],
        compiler_params=pltpu.CompilerParams(vmem_limit_bytes=8 << 20),
        name="load",
    )(*[pltpu.with_memory_space_constraint(mat, pltpu.HBM) for mat in mats])


def join_kernel(*refs):
    at = 0
    for ref in refs[:-1]:
        refs[-1][pl.ds(at, ref.shape[0]), :] = ref[...]
        at += ref.shape[0]


def join(*parts):
    rows = sum(x.shape[0] for x in parts)
    shape = jax.ShapeDtypeStruct((rows, parts[0].shape[1]), parts[0].dtype)
    return local(join_kernel, shape, *parts, name="join")


def add_kernel(*refs, count):
    total = refs[0][...].astype(jnp.float32)
    for ref in refs[1:count]:
        total = total + ref[...].astype(jnp.float32)
    at = 0
    for out in refs[count:]:
        out[...] = total[at : at + out.shape[0]].astype(out.dtype)
        at += out.shape[0]


def add(operands, *outs):
    shapes = [jax.ShapeDtypeStruct((rows, operands[0].shape[1]), dtype) for rows, dtype in outs]
    kernel = functools.partial(add_kernel, count=len(operands))
    return local(kernel, shapes, *operands, name="add")


def finish_kernel(stream_ref, own_ref, *rest):
    arrived, out_ref = rest[:-1], rest[-1]
    total = stream_ref[...] + own_ref[...]
    for ref in arrived:
        total = total + ref[...].astype(jnp.float32)
    steps, each, _ = out_ref.shape
    for t in range(steps):
        out_ref[t] = total[t * each : (t + 1) * each].astype(jnp.bfloat16)


def experts_kernel(place, spot, ids_ref, route_ref, gate, up, down, *refs, plan):
    count = len(plan)
    ring, width, bits = plan[0][:3]
    top, steps, requests = ids_ref.shape
    each = requests // (ring * width)
    size = steps * each
    routes = [route_ref[k] for k in range(top)]
    norm = functools.reduce(jnp.add, routes)
    own = spot[0] * ring + place[0]
    picked = jnp.zeros((steps, requests), jnp.float32)
    for k in range(top):
        picked = picked + jnp.where(ids_ref[k] == own, routes[k] / norm, 0.0)

    rows_ref = refs[-1]
    at = 0
    shares = []
    for (_, _, _, flip, skip), x_ref in zip(plan, refs[:count]):
        rows = x_ref.shape[0]
        rows_ref[pl.ds(at, rows), :] = x_ref[...]
        at += rows
        row = lax.broadcasted_iota(jnp.int32, (rows, requests), 0) + skip
        column = lax.broadcasted_iota(jnp.int32, (rows, requests), 1)
        block = row // size
        k, m = block % ring, block // ring
        device = jnp.bitwise_xor(spot[0], flip)
        core = device % 2
        mask = jnp.zeros_like(row)
        for j in range(bits):
            mask = mask + ((m >> j) & 1) * (jnp.int32(2) << ((j + core) % bits))
        far = place[0] + k
        far = jnp.where(far >= ring, far - ring, far)
        owner = jnp.bitwise_xor(device, mask) * ring + far
        moment = (row % size) // each
        request = owner * each + row % each
        share = jnp.zeros((rows, requests), jnp.float32)
        for t in range(steps):
            share = jnp.where(moment == t, jnp.broadcast_to(picked[t : t + 1], (rows, requests)), share)
        shares.append(jnp.sum(jnp.where(request == column, share, 0.0), axis=-1, keepdims=True))

    x = rows_ref[...]
    gated = jnp.dot(x, gate[...], preferred_element_type=jnp.float32)
    lifted = jnp.dot(x, up[...], preferred_element_type=jnp.float32)
    hidden = (jax.nn.silu(gated) * lifted).astype(jnp.bfloat16)
    served = jnp.dot(hidden, down[...], preferred_element_type=jnp.float32)
    served = served.astype(jnp.bfloat16).astype(jnp.float32)
    at = 0
    for share, out_ref in zip(shares, refs[count : 2 * count]):
        rows = out_ref.shape[0]
        out_ref[...] = (served[at : at + rows] * share).astype(out_ref.dtype)
        at += rows


def shards(
    queries,
    keys_in,
    values_in,
    out_gate,
    beta_logit,
    decay_rate,
    states,
    out_weight,
    head_gain,
    residual,
    post_gain,
    expert_ids,
    route_weight,
    expert_gate,
    expert_up,
    expert_down,
):
    ring, width = lax.axis_size("head"), lax.axis_size("dev")
    place = lax.axis_index("head").astype(jnp.int32).reshape(1)
    spot = lax.axis_index("dev").astype(jnp.int32).reshape(1)
    steps, each, columns = residual.shape
    size = steps * each
    bits = (width // 2).bit_length() - 1

    def along(x, k):
        return lax.ppermute(x, "head", [(i, (i + k) % ring) for i in range(ring)])

    def across(x, j):
        return lax.ppermute(
            x, "dev", [(i, i ^ (2 << ((j + i % 2) % bits))) for i in range(width)]
        )

    def other(x):
        return lax.ppermute(x, "dev", [(i, i ^ 1) for i in range(width)])

    parts = attend(
        place,
        spot,
        queries,
        keys_in,
        values_in,
        out_gate,
        beta_logit.transpose(0, 2, 1),
        decay_rate.transpose(0, 2, 1),
        head_gain.reshape(1, HV),
        states,
        out_weight,
        ring,
    )
    arrived = [along(parts[k], k) for k in range(1, ring)]
    arrived, weights = lax.optimization_barrier(
        (arrived, load(expert_gate, expert_up, expert_down))
    )
    stream, normed = local(
        norm_kernel,
        [
            jax.ShapeDtypeStruct((size, columns), jnp.float32),
            jax.ShapeDtypeStruct((size, columns), jnp.bfloat16),
        ],
        parts[0],
        residual,
        post_gain.reshape(1, columns),
        *arrived,
        name="norm",
    )

    ids, route = expert_ids.transpose(2, 0, 1), route_weight.transpose(2, 0, 1)

    def experts(*pieces):
        return local(
            functools.partial(
                experts_kernel,
                plan=tuple((ring, width, bits, flip, skip) for _, _, flip, skip in pieces),
            ),
            [jax.ShapeDtypeStruct(x.shape, dtype) for x, dtype, _, _ in pieces],
            place,
            spot,
            ids,
            route,
            *weights,
            *[x for x, _, _, _ in pieces],
            name="experts",
            scratch=[pltpu.VMEM((sum(x.shape[0] for x, _, _, _ in pieces), columns), jnp.bfloat16)],
        )

    blocks = [normed] + [along(normed, ring - k) for k in range(1, ring)]
    firsts = [join(*blocks[: ring // 2]), join(*blocks[ring // 2 :])]
    first = join(*firsts)
    held = first.shape[0]
    last = (1 << bits) - 1
    sets, parts, served, totals = {0: first}, {0: firsts}, {}, {}

    def serve(m, peers):
        served[m] = experts((sets[m], jnp.float32, 0, m * held), (peers, jnp.bfloat16, 1, m * held))

    later = first
    for j in range(bits):
        top = 1 << j
        if j < bits - 1 or j == 0:
            parts[top] = [across(x, j) for x in parts[0]]
        else:
            sets[top] = across(later, j)
        if j == 0:
            serve(0, other(first))
            later, served[0], parts[1] = lax.optimization_barrier((first, served[0], parts[1]))
            later = first
        for m in range(1, top):
            parts[m + top] = [across(x, j) for x in parts[m]]
            if m not in served:
                peers = other(sets[m])
                if top in sets:
                    peers, sets[top] = lax.optimization_barrier((peers, sets[top]))
                serve(m, peers)
                parts[m + top], served[m] = lax.optimization_barrier((parts[m + top], served[m]))
        for m in range(1, 2 * top):
            if m not in sets:
                sets[m] = join(*parts[m])
    for m in range(1 << (bits - 1), last + 1):
        peers = other(sets[m])
        if m > 1 and m - 1 in served:
            peers, served[m - 1] = lax.optimization_barrier((peers, served[m - 1]))
        serve(m, peers)
    for m in range(last + 1):
        leaves = m >> (bits - 1)
        totals[m] = add(
            (served[m][0], other(served[m][1])), (held, jnp.bfloat16 if leaves else jnp.float32)
        )[0]
    came = {}
    for j in reversed(range(bits)):
        top = 1 << j
        for m in reversed(range(1, top)):
            leaves = m >> (j - 1)
            totals[m] = add(
                (totals[m], across(totals[m + top], j)),
                (held, jnp.bfloat16 if leaves else jnp.float32),
            )[0]
        if top > 1:
            totals[top], totals[0] = lax.optimization_barrier((totals[top], totals[0]))
        came[j] = across(totals[top], j)
    total, *blocks = add(
        (totals[0], *[came[j] for j in reversed(range(bits))]),
        (size, jnp.float32),
        *[(size, jnp.bfloat16)] * (ring - 1),
    )
    return local(
        finish_kernel,
        jax.ShapeDtypeStruct((steps, each, columns), jnp.bfloat16),
        stream,
        total,
        *[along(x, k + 1) for k, x in enumerate(blocks)],
        name="finish",
    )


def solution(mesh):
    return jax.shard_map(
        shards,
        mesh=mesh,
        in_specs=(
            P(None, ("groups", "dev"), "head"),
            P(None, ("groups", "dev"), "head"),
            P(None, ("groups", "dev"), "head"),
            P(None, ("groups", "dev"), "head"),
            P(None, ("groups", "dev"), "head"),
            P(None, ("groups", "dev"), "head"),
            P(("groups", "dev"), "head", None, None),
            P("head", None),
            P(),
            P(None, ("groups", "dev", "head"), None),
            P(),
            P(None, "groups", None),
            P(None, "groups", None),
            P(("dev", "head"), None, None),
            P(("dev", "head"), None, None),
            P(("dev", "head"), None, None),
        ),
        out_specs=P(None, ("groups", "dev", "head"), None),
        check_vma=False,
    )
```

```python
import functools

import jax
import jax.numpy as jnp
from jax import lax
from jax.experimental import pallas as pl
from jax.experimental.pallas import tpu as pltpu
from jax.sharding import PartitionSpec as P

HK = 128
HV = 128
EPS = 1e-06
AHEAD = 3


def attend_kernel(place, spot, *refs, blocks):
    q_hbm, k_hbm, v_hbm, gate_hbm, beta_hbm, decay_hbm, gain_hbm, states_hbm, weight_hbm = refs[:9]
    refs = refs[9:]
    own_ref, send_refs = refs[0], refs[1:blocks]
    (q_ref, k_ref, v_ref, gate_ref, beta_ref, decay_ref, gain_ref, state, weight) = refs[
        blocks : blocks + 9
    ]
    rows, reads, gated, small_sems, state_sems, weight_sems = refs[blocks + 9 :]
    steps, requests, _ = q_ref.shape
    heads = v_ref.shape[2] // HV
    pairs = q_ref.shape[2] // HK
    repeat = heads // pairs
    each = requests // blocks
    vectors = 2 * steps

    small = [
        pltpu.make_async_copy(src, dst, small_sems.at[i])
        for i, (src, dst) in enumerate(
            (
                (q_hbm, q_ref),
                (k_hbm, k_ref),
                (v_hbm, v_ref),
                (gate_hbm, gate_ref),
                (beta_hbm, beta_ref),
                (decay_hbm, decay_ref),
                (gain_hbm, gain_ref),
            )
        )
    ]
    large = pltpu.make_async_copy(weight_hbm, weight, weight_sems.at[0])
    for copy in small[:2]:
        copy.start()
    parts = [
        pltpu.make_async_copy(
            states_hbm.at[:, pl.ds(g * repeat, repeat)],
            state.at[:, pl.ds(g * repeat, repeat)],
            state_sems.at[g],
        )
        for g in range(pairs)
    ]
    parts[0].start()
    for copy in small[2:]:
        copy.start()
    for copy in parts[1:AHEAD]:
        copy.start()
    for copy in small[:2]:
        copy.wait()

    unit_q, unit_k = {}, {}
    for g in range(pairs):
        lanes = slice(g * HK, (g + 1) * HK)
        for t in range(steps):
            q = q_ref[t, :, lanes].astype(jnp.float32)
            k = k_ref[t, :, lanes].astype(jnp.float32)
            q = q * lax.rsqrt(jnp.sum(q * q, axis=-1, keepdims=True) + EPS) * HK ** (-0.5)
            k = k * lax.rsqrt(jnp.sum(k * k, axis=-1, keepdims=True) + EPS)
            for i, value in ((t, q), (steps + t, k)):
                high = value.astype(jnp.bfloat16).astype(jnp.float32)
                rows[g, pl.ds(i, requests, stride=2 * vectors), :] = high
                rows[g, pl.ds(vectors + i, requests, stride=2 * vectors), :] = value - high
            unit_q[g, t], unit_k[g, t] = q, k

    def read_states(g, r, carry):
        both = pl.ds(pl.multiple_of(r * 2 * vectors, 2 * vectors), 2 * vectors)
        at = pl.ds(pl.multiple_of(r * vectors, vectors), vectors)
        left = rows[g, both, :].astype(jnp.bfloat16)
        right = [state[r, g * repeat + i].astype(jnp.bfloat16) for i in range(repeat)]
        read = jnp.dot(left, jnp.concatenate(right, axis=1), preferred_element_type=jnp.float32)
        read = read[:vectors] + read[vectors:]
        for i in range(repeat):
            reads[g * repeat + i, at, :] = read[:, i * HV : (i + 1) * HV]
        return carry

    for copy in small[2:]:
        copy.wait()
    betas = jax.nn.sigmoid(beta_ref[...].reshape(steps * heads, requests).T)
    decays = decay_ref[...].reshape(steps * heads, requests).T
    for g in range(pairs):
        parts[g].wait()
        if g + AHEAD < pairs:
            parts[g + AHEAD].start()
        if g == max(pairs - AHEAD, 0):
            large.start()
        lax.fori_loop(0, requests, functools.partial(read_states, g), 0, unroll=True)
        kk, qk = {}, {}
        for t in range(steps):
            for s in range(t + 1):
                qk[t, s] = jnp.sum(unit_q[g, t] * unit_k[g, s], axis=-1, keepdims=True)
                if s < t:
                    kk[t, s] = jnp.sum(unit_k[g, t] * unit_k[g, s], axis=-1, keepdims=True)
        for h in range(g * repeat, (g + 1) * repeat):
            lanes = slice(h * HV, (h + 1) * HV)
            decay = [decays[:, t * heads + h : t * heads + h + 1] for t in range(steps)]
            span = {}
            for t in range(steps):
                span[t, t] = None
                for s in range(t - 1, -2, -1):
                    last = span[t, s + 1]
                    span[t, s] = decay[s + 1] if last is None else last * decay[s + 1]
            deltas = []
            for t in range(steps):
                start_q = reads[h, pl.ds(t, requests, stride=vectors), :]
                start_k = reads[h, pl.ds(steps + t, requests, stride=vectors), :]
                recalled = span[t, -1] * start_k
                for s in range(t):
                    recalled = recalled + (span[t, s] * kk[t, s]) * deltas[s]
                beta = betas[:, t * heads + h : t * heads + h + 1]
                deltas.append((v_ref[t, :, lanes].astype(jnp.float32) - recalled) * beta)
                read = span[t, -1] * start_q
                for s in range(t + 1):
                    factor = qk[t, s] if s == t else span[t, s] * qk[t, s]
                    read = read + factor * deltas[s]
                scale = lax.rsqrt(jnp.mean(read * read, axis=-1, keepdims=True) + EPS)
                gate = gate_ref[t, :, lanes].astype(jnp.float32)
                value = read * scale * gain_ref[...] * jax.nn.silu(gate)
                gated[pl.ds(t * requests, requests), lanes] = value.astype(jnp.bfloat16)

    total = steps * requests
    new = lax.broadcasted_iota(jnp.int32, (total, total), 0)
    old = lax.broadcasted_iota(jnp.int32, (total, total), 1)
    block = new // (steps * each) + place[0]
    block = jnp.where(block >= blocks, block - blocks, block)
    within = new % (steps * each)
    source = (within // each) * requests + block * each + within % each
    chosen = jnp.where(source == old, 1.0, 0.0).astype(jnp.bfloat16)
    ordered = jnp.dot(chosen, gated[...], preferred_element_type=jnp.float32).astype(jnp.bfloat16)

    large.wait()
    size = steps * each
    columns = weight.shape[1]
    tile = min(512, columns)
    for c in range(0, columns, tile):
        part = jnp.dot(ordered, weight[:, c : c + tile], preferred_element_type=jnp.float32)
        own_ref[:, c : c + tile] = part[:size]
        for k in range(1, blocks):
            send_refs[k - 1][:, c : c + tile] = part[k * size : (k + 1) * size].astype(jnp.bfloat16)


def attend(place, spot, queries, keys_in, values_in, out_gate, beta, decay, gain, states, weight, blocks):
    steps, requests, _ = queries.shape
    heads = values_in.shape[2] // HV
    pairs = queries.shape[2] // HK
    size = steps * requests // blocks
    columns = weight.shape[1]
    whole = pl.BlockSpec(memory_space=pltpu.VMEM)
    far = pl.BlockSpec(memory_space=pltpu.HBM)
    small = (queries, keys_in, values_in, out_gate, beta, decay, gain)
    return pl.pallas_call(
        functools.partial(attend_kernel, blocks=blocks),
        out_shape=[jax.ShapeDtypeStruct((size, columns), jnp.float32)]
        + [jax.ShapeDtypeStruct((size, columns), jnp.bfloat16)] * (blocks - 1),
        in_specs=[pl.BlockSpec(memory_space=pltpu.SMEM)] * 2 + [far] * 9,
        out_specs=[whole] * blocks,
        scratch_shapes=[pltpu.VMEM(x.shape, x.dtype) for x in small]
        + [
            pltpu.VMEM(states.shape, jnp.float32),
            pltpu.VMEM(weight.shape, jnp.bfloat16),
            pltpu.VMEM((pairs, requests * 4 * steps, HK), jnp.float32),
            pltpu.VMEM((heads, requests * 2 * steps, HV), jnp.float32),
            pltpu.VMEM((steps * requests, heads * HV), jnp.bfloat16),
            pltpu.SemaphoreType.DMA((len(small),)),
            pltpu.SemaphoreType.DMA((pairs,)),
            pltpu.SemaphoreType.DMA((1,)),
        ],
        compiler_params=pltpu.CompilerParams(vmem_limit_bytes=32 << 20),
        name="attend",
    )(place, spot, *[pltpu.with_memory_space_constraint(x, pltpu.HBM) for x in (*small, states, weight)])


def local(kernel, out_shape, *operands, name, scratch=()):
    whole = pl.BlockSpec(memory_space=pltpu.VMEM)
    scalars = [x.ndim == 1 for x in operands]
    return pl.pallas_call(
        kernel,
        out_shape=out_shape,
        in_specs=[pl.BlockSpec(memory_space=pltpu.SMEM) if one else whole for one in scalars],
        out_specs=jax.tree.map(lambda _: whole, out_shape),
        compiler_params=pltpu.CompilerParams(vmem_limit_bytes=12 << 20),
        scratch_shapes=scratch,
        name=name,
    )(*operands)


def norm_kernel(own_ref, residual_ref, gain_ref, *rest):
    arrived, (stream_ref, normed_ref) = rest[:-2], rest[-2:]
    steps, each, _ = residual_ref.shape
    for t in range(steps):
        at = slice(t * each, (t + 1) * each)
        stream_ref[at, :] = residual_ref[t].astype(jnp.float32)
    stream = stream_ref[...] + own_ref[...]
    for ref in arrived:
        stream = stream + ref[...].astype(jnp.float32)
    stream_ref[...] = stream
    scale = lax.rsqrt(jnp.mean(stream * stream, axis=-1, keepdims=True) + EPS)
    normed_ref[...] = (stream * scale * gain_ref[...]).astype(jnp.bfloat16)


def load_kernel(*refs):
    count = len(refs) // 2
    copies = [
        pltpu.make_async_copy(src.at[0], dst, refs[-1].at[i])
        for i, (src, dst) in enumerate(zip(refs[:count], refs[count:-1]))
    ]
    for copy in copies:
        copy.start()
    for copy in copies:
        copy.wait()


def load(*mats):
    return pl.pallas_call(
        load_kernel,
        out_shape=[jax.ShapeDtypeStruct(mat.shape[1:], mat.dtype) for mat in mats],
        in_specs=[pl.BlockSpec(memory_space=pltpu.HBM)] * len(mats),
        out_specs=[pl.BlockSpec(memory_space=pltpu.VMEM)] * len(mats),
        scratch_shapes=[pltpu.SemaphoreType.DMA((len(mats),))],
        compiler_params=pltpu.CompilerParams(vmem_limit_bytes=8 << 20),
        name="load",
    )(*[pltpu.with_memory_space_constraint(mat, pltpu.HBM) for mat in mats])


def join_kernel(*refs):
    at = 0
    for ref in refs[:-1]:
        refs[-1][pl.ds(at, ref.shape[0]), :] = ref[...]
        at += ref.shape[0]


def join(*parts):
    rows = sum(x.shape[0] for x in parts)
    shape = jax.ShapeDtypeStruct((rows, parts[0].shape[1]), parts[0].dtype)
    return local(join_kernel, shape, *parts, name="join")


def add_kernel(*refs, count):
    total = refs[0][...].astype(jnp.float32)
    for ref in refs[1:count]:
        total = total + ref[...].astype(jnp.float32)
    at = 0
    for out in refs[count:]:
        out[...] = total[at : at + out.shape[0]].astype(out.dtype)
        at += out.shape[0]


def add(operands, *outs):
    shapes = [jax.ShapeDtypeStruct((rows, operands[0].shape[1]), dtype) for rows, dtype in outs]
    kernel = functools.partial(add_kernel, count=len(operands))
    return local(kernel, shapes, *operands, name="add")


def finish_kernel(stream_ref, own_ref, *rest):
    arrived, out_ref = rest[:-1], rest[-1]
    total = stream_ref[...] + own_ref[...]
    for ref in arrived:
        total = total + ref[...].astype(jnp.float32)
    steps, each, _ = out_ref.shape
    for t in range(steps):
        out_ref[t] = total[t * each : (t + 1) * each].astype(jnp.bfloat16)


def experts_kernel(place, spot, ids_ref, route_ref, gate, up, down, *refs, plan):
    count = len(plan)
    ring, width, bits = plan[0][:3]
    top, steps, requests = ids_ref.shape
    each = requests // (ring * width)
    size = steps * each
    routes = [route_ref[k] for k in range(top)]
    norm = functools.reduce(jnp.add, routes)
    own = spot[0] * ring + place[0]
    picked = jnp.zeros((steps, requests), jnp.float32)
    for k in range(top):
        picked = picked + jnp.where(ids_ref[k] == own, routes[k] / norm, 0.0)

    rows_ref = refs[-1]
    at = 0
    shares = []
    for (_, _, _, flip, skip), x_ref in zip(plan, refs[:count]):
        rows = x_ref.shape[0]
        rows_ref[pl.ds(at, rows), :] = x_ref[...]
        at += rows
        row = lax.broadcasted_iota(jnp.int32, (rows, requests), 0) + skip
        column = lax.broadcasted_iota(jnp.int32, (rows, requests), 1)
        block = row // size
        k, m = block % ring, block // ring
        device = jnp.bitwise_xor(spot[0], flip)
        core = device % 2
        mask = jnp.zeros_like(row)
        for j in range(bits):
            mask = mask + ((m >> j) & 1) * (jnp.int32(2) << ((j + core) % bits))
        far = place[0] + k
        far = jnp.where(far >= ring, far - ring, far)
        owner = jnp.bitwise_xor(device, mask) * ring + far
        moment = (row % size) // each
        request = owner * each + row % each
        share = jnp.zeros((rows, requests), jnp.float32)
        for t in range(steps):
            share = jnp.where(moment == t, jnp.broadcast_to(picked[t : t + 1], (rows, requests)), share)
        shares.append(jnp.sum(jnp.where(request == column, share, 0.0), axis=-1, keepdims=True))

    x = rows_ref[...]
    gated = jnp.dot(x, gate[...], preferred_element_type=jnp.float32)
    lifted = jnp.dot(x, up[...], preferred_element_type=jnp.float32)
    hidden = (jax.nn.silu(gated) * lifted).astype(jnp.bfloat16)
    served = jnp.dot(hidden, down[...], preferred_element_type=jnp.float32)
    served = served.astype(jnp.bfloat16).astype(jnp.float32)
    at = 0
    for share, out_ref in zip(shares, refs[count : 2 * count]):
        rows = out_ref.shape[0]
        out_ref[...] = (served[at : at + rows] * share).astype(out_ref.dtype)
        at += rows


def shards(
    queries,
    keys_in,
    values_in,
    out_gate,
    beta_logit,
    decay_rate,
    states,
    out_weight,
    head_gain,
    residual,
    post_gain,
    expert_ids,
    route_weight,
    expert_gate,
    expert_up,
    expert_down,
):
    ring, width = lax.axis_size("head"), lax.axis_size("dev")
    place = lax.axis_index("head").astype(jnp.int32).reshape(1)
    spot = lax.axis_index("dev").astype(jnp.int32).reshape(1)
    steps, each, columns = residual.shape
    size = steps * each
    bits = (width // 2).bit_length() - 1

    def along(x, k):
        return lax.ppermute(x, "head", [(i, (i + k) % ring) for i in range(ring)])

    def across(x, j):
        return lax.ppermute(
            x, "dev", [(i, i ^ (2 << ((j + i % 2) % bits))) for i in range(width)]
        )

    def other(x):
        return lax.ppermute(x, "dev", [(i, i ^ 1) for i in range(width)])

    parts = attend(
        place,
        spot,
        queries,
        keys_in,
        values_in,
        out_gate,
        beta_logit.transpose(0, 2, 1),
        decay_rate.transpose(0, 2, 1),
        head_gain.reshape(1, HV),
        states,
        out_weight,
        ring,
    )
    arrived = [along(parts[k], k) for k in range(1, ring)]
    arrived, weights = lax.optimization_barrier(
        (arrived, load(expert_gate, expert_up, expert_down))
    )
    stream, normed = local(
        norm_kernel,
        [
            jax.ShapeDtypeStruct((size, columns), jnp.float32),
            jax.ShapeDtypeStruct((size, columns), jnp.bfloat16),
        ],
        parts[0],
        residual,
        post_gain.reshape(1, columns),
        *arrived,
        name="norm",
    )

    ids, route = expert_ids.transpose(2, 0, 1), route_weight.transpose(2, 0, 1)

    def experts(*pieces):
        return local(
            functools.partial(
                experts_kernel,
                plan=tuple((ring, width, bits, flip, skip) for _, _, flip, skip in pieces),
            ),
            [jax.ShapeDtypeStruct(x.shape, dtype) for x, dtype, _, _ in pieces],
            place,
            spot,
            ids,
            route,
            *weights,
            *[x for x, _, _, _ in pieces],
            name="experts",
            scratch=[pltpu.VMEM((sum(x.shape[0] for x, _, _, _ in pieces), columns), jnp.bfloat16)],
        )

    blocks = [normed] + [along(normed, ring - k) for k in range(1, ring)]
    firsts = [join(*blocks[: ring // 2]), join(*blocks[ring // 2 :])]
    first = join(*firsts)
    held = first.shape[0]
    last = (1 << bits) - 1
    sets, parts, served, totals = {0: first}, {0: firsts}, {}, {}

    def serve(m, peers):
        served[m] = experts((sets[m], jnp.float32, 0, m * held), (peers, jnp.bfloat16, 1, m * held))

    later = first
    for j in range(bits):
        top = 1 << j
        if j < bits - 1 or j == 0:
            parts[top] = [across(x, j) for x in parts[0]]
        else:
            sets[top] = across(later, j)
        if j == 0:
            serve(0, other(first))
            later, served[0], parts[1] = lax.optimization_barrier((first, served[0], parts[1]))
            later = first
        for m in range(1, top):
            parts[m + top] = [across(x, j) for x in parts[m]]
            if m not in served:
                peers = other(sets[m])
                if top in sets:
                    peers, sets[top] = lax.optimization_barrier((peers, sets[top]))
                serve(m, peers)
                parts[m + top], served[m] = lax.optimization_barrier((parts[m + top], served[m]))
        for m in range(1, 2 * top):
            if m not in sets:
                sets[m] = join(*parts[m])
    for m in range(1 << (bits - 1), last + 1):
        peers = other(sets[m])
        if m > 1 and m - 1 in served:
            peers, served[m - 1] = lax.optimization_barrier((peers, served[m - 1]))
        serve(m, peers)
    cut = 2
    for m in range(last + 1):
        leaves = m >> (bits - 1)
        kind = jnp.bfloat16 if leaves else jnp.float32
        pieces = cut if m % 2 else 1
        totals[m] = add((served[m][0], other(served[m][1])), *[(held // pieces, kind)] * pieces)
    came = {}
    for j in reversed(range(bits)):
        top = 1 << j
        for m in reversed(range(1, top)):
            kind = jnp.bfloat16 if m >> (j - 1) else jnp.float32
            totals[m] = [
                add((x, across(y, j)), (x.shape[0], kind))[0]
                for x, y in zip(totals[m], totals[m + top])
            ]
        if top > 1:
            totals[top], totals[0] = lax.optimization_barrier((totals[top], totals[0]))
        sent = [across(x, j) for x in totals[top]]
        came[j] = join(*sent) if len(sent) > 1 else sent[0]
    total, *blocks = add(
        (totals[0][0], *[came[j] for j in reversed(range(bits))]),
        (size, jnp.float32),
        *[(size, jnp.bfloat16)] * (ring - 1),
    )
    return local(
        finish_kernel,
        jax.ShapeDtypeStruct((steps, each, columns), jnp.bfloat16),
        stream,
        total,
        *[along(x, k + 1) for k, x in enumerate(blocks)],
        name="finish",
    )


def solution(mesh):
    return jax.shard_map(
        shards,
        mesh=mesh,
        in_specs=(
            P(None, ("groups", "dev"), "head"),
            P(None, ("groups", "dev"), "head"),
            P(None, ("groups", "dev"), "head"),
            P(None, ("groups", "dev"), "head"),
            P(None, ("groups", "dev"), "head"),
            P(None, ("groups", "dev"), "head"),
            P(("groups", "dev"), "head", None, None),
            P("head", None),
            P(),
            P(None, ("groups", "dev", "head"), None),
            P(),
            P(None, "groups", None),
            P(None, "groups", None),
            P(("dev", "head"), None, None),
            P(("dev", "head"), None, None),
            P(("dev", "head"), None, None),
        ),
        out_specs=P(None, ("groups", "dev", "head"), None),
        check_vma=False,
    )
```
